32 devices in a mesh: group: 2 (over x), fsdp: 16 (over z, y, core).
Axes of the slice: x: 2, y: 2, z: 4, core: 2. Of those that a mesh axis runs over, the one named last changes fastest.
Arguments:
- acts: bfloat16 [4096, 8192], P(('group', 'fsdp')), parts along dimension 0, may hold values from -6 to 6
- cotangent: bfloat16 [4096, 8192], P(('group', 'fsdp')), parts along dimension 0, may hold values from -6 to 6
- down_weight_slots: bfloat16 [16, 16, 8192], P('fsdp'), may hold values from -0.25 to 0.25
- up_weight_slots: bfloat16 [16, 16, 8192], P('fsdp'), may hold values from -0.125 to 0.125
- adapter_per_tile: int32 [32], P(('group', 'fsdp')), parts along dimension 0, may hold values from 0 to 15, each once
- adapter_storage_slot: int32 [16], replicated, may hold values from 0 to 15, each once
Outputs:
- grad_acts: bfloat16 [4096, 8192], P(('group', 'fsdp')), parts along dimension 0
- grad_a: bfloat16 [32, 16, 8192], P(('group', 'fsdp')), parts along dimension 0
- grad_b: bfloat16 [32, 16, 8192], P(('group', 'fsdp')), parts along dimension 0
The draws below stay inside these ranges and needn't reach their ends.
There are 2 independent parts, one for each index of `group`. The reference program is written for one: setup_inputs(seed, part) draws one part's arguments, and reference() takes and returns one part's arrays. A program takes and returns all parts, laid end to end along the dimension named above; an argument that names none is the same for every part. Nothing has to cross between parts.
Inputs may be any that keep to these rules, and one draw needn't show every extreme that they name: `adapter_per_tile`: within each group's 16 entries every adapter appears exactly once. `adapter_storage_slot`: every slot holds exactly one adapter.
All inputs are finite; a program needn't handle non-finite values.
Results may differ from the reference program's by a relative error of at most 0.005.
Values may be sent and summed in bfloat16 or wider, within the bound.
No kernel may reach another device: no remote copies, remote signals or barrier semaphores. Data moves between devices by JAX's collectives and lax.ppermute only.
A program may use at most 64 MiB of HBM per device.

```python
import jax
import jax.numpy as jnp

MODEL_WIDTH = 8192
ADAPTER_RANK = 16
TILE = 128
TILES = 16
TOKENS = 2048
ADAPTER_COUNT = 16


def level_of(key, shape, pieces, smallest, top_value):
    factor_of, own = 1.0, jax.random.fold_in(key, 6)
    for position, shards_of in pieces:
        heights = jnp.exp(jax.random.uniform(jax.random.fold_in(own, position), (shards_of,), jnp.float32, smallest / len(pieces), top_value / len(pieces)))
        factor_of = factor_of * jnp.repeat(heights, shape[position] // shards_of).reshape([-1 if axis == position else 1 for axis in range(len(shape))])
    return factor_of


def normal_values(key, dims, spread, limit, split=(), kind=jnp.bfloat16):
    factor_of = level_of(key, dims, split, -0.22, 0.18) if split else 1.0
    values = jax.random.normal(key, dims, jnp.float32) * spread * factor_of
    return jnp.minimum(jnp.maximum(values, -limit), limit).astype(kind)


def setup_inputs(seed: int = 0, part: int = 0) -> dict:
    splits = jax.random.split(jax.random.key(seed), 7)
    part_splits = jax.random.split(jax.random.fold_in(splits[6], part), 7)
    return {
        "acts": normal_values(part_splits[0], (TOKENS, MODEL_WIDTH), 1.0, 6.0, ((0, 16),)),
        "cotangent": normal_values(part_splits[1], (TOKENS, MODEL_WIDTH), 1.0, 6.0, ((0, 16),)),
        "down_weight_slots": normal_values(splits[2], (ADAPTER_COUNT, ADAPTER_RANK, MODEL_WIDTH), 512 ** -0.5, 0.25, ((0, 16),)),
        "up_weight_slots": normal_values(splits[3], (ADAPTER_COUNT, ADAPTER_RANK, MODEL_WIDTH), 2048 ** -0.5, 0.125, ((0, 16),)),
        "adapter_per_tile": jax.random.permutation(part_splits[4], ADAPTER_COUNT).astype(jnp.int32),
        "adapter_storage_slot": jax.random.permutation(splits[5], ADAPTER_COUNT).astype(jnp.int32),
    }


def reference(acts, cotangent, down_weight_slots, up_weight_slots, adapter_per_tile, adapter_storage_slot):
    storage_index = adapter_storage_slot[adapter_per_tile].astype(jnp.int32)
    xs = acts.reshape(TILES, TILE, MODEL_WIDTH).astype(jnp.float32)
    gs = cotangent.reshape(TILES, TILE, MODEL_WIDTH).astype(jnp.float32)
    down_factor = down_weight_slots[storage_index].astype(jnp.float32)
    up_factor = up_weight_slots[storage_index].astype(jnp.float32)
    low_u = jnp.einsum('tkd,trd->trk', xs, down_factor).astype(jnp.bfloat16).astype(jnp.float32)
    low_h = jnp.einsum('tkd,trd->trk', gs, up_factor).astype(jnp.bfloat16).astype(jnp.float32)
    grad_x = jnp.einsum('trk,trd->tkd', low_h, down_factor).astype(jnp.bfloat16).reshape(TOKENS, MODEL_WIDTH)
    tile_ga = jnp.einsum('trk,tkd->trd', low_h, xs)
    tile_gb = jnp.einsum('trk,tkd->trd', low_u, gs)
    grad_a = jnp.zeros((ADAPTER_COUNT, ADAPTER_RANK, MODEL_WIDTH), jnp.float32).at[storage_index].add(tile_ga)
    grad_b = jnp.zeros((ADAPTER_COUNT, ADAPTER_RANK, MODEL_WIDTH), jnp.float32).at[storage_index].add(tile_gb)
    return grad_x, grad_a.astype(jnp.bfloat16), grad_b.astype(jnp.bfloat16)
```

```python
import functools

import jax
import jax.numpy as jnp
from jax import lax
from jax.experimental import pallas as pl
from jax.experimental.pallas import tpu as pltpu
from jax.sharding import PartitionSpec as P

F32 = jnp.float32
VMEM_LIMIT = 48 * 1024 * 1024


def pack_kernel(down_ref, up_ref, out_ref):
    n, _, w = out_ref.shape
    r = down_ref.shape[1]
    for j in range(n):
        out_ref[j, 0:r, :] = down_ref[0, :, j * w : (j + 1) * w]
        out_ref[j, r : 2 * r, :] = up_ref[0, :, j * w : (j + 1) * w]


def pack(down, up, n):
    _, r, d = down.shape
    return pl.pallas_call(
        pack_kernel,
        out_shape=jax.ShapeDtypeStruct((n, 2 * r, d // n), down.dtype),
        compiler_params=pltpu.CompilerParams(vmem_limit_bytes=VMEM_LIMIT),
    )(down, up)


def unpack_kernel(in_ref, ga_ref, gb_ref):
    n, _, w = in_ref.shape
    r = ga_ref.shape[1]
    for j in range(n):
        ga_ref[0, :, j * w : (j + 1) * w] = in_ref[j, 0:r, :]
        gb_ref[0, :, j * w : (j + 1) * w] = in_ref[j, r : 2 * r, :]


def unpack(blocks):
    n, r2, w = blocks.shape
    out = jax.ShapeDtypeStruct((1, r2 // 2, n * w), blocks.dtype)
    return pl.pallas_call(
        unpack_kernel,
        out_shape=(out, out),
        compiler_params=pltpu.CompilerParams(vmem_limit_bytes=VMEM_LIMIT),
    )(blocks)


def permute_kernel(index_ref, in_ref, out_ref):
    n = out_ref.shape[0]
    for t in range(n):
        out_ref[t] = in_ref[index_ref[t]]


def permute(index, blocks):
    return pl.pallas_call(
        permute_kernel,
        out_shape=jax.ShapeDtypeStruct(blocks.shape, blocks.dtype),
        in_specs=[
            pl.BlockSpec(memory_space=pltpu.SMEM),
            pl.BlockSpec(memory_space=pltpu.VMEM),
        ],
        compiler_params=pltpu.CompilerParams(vmem_limit_bytes=VMEM_LIMIT),
    )(index, blocks)


def grads_kernel(acts_ref, cot_ref, fac_ref, gx_ref, out_ref):
    n, r2, w = fac_ref.shape
    r = r2 // 2
    rows = acts_ref.shape[0]
    dims_nt = (((1,), (1,)), ((), ()))
    low_u = jnp.zeros((r, rows), F32)
    low_h = jnp.zeros((r, rows), F32)
    for j in range(n):
        cols = slice(j * w, (j + 1) * w)
        low_u += lax.dot_general(fac_ref[j, 0:r, :], acts_ref[:, cols], dims_nt, preferred_element_type=F32)
        low_h += lax.dot_general(fac_ref[j, r:r2, :], cot_ref[:, cols], dims_nt, preferred_element_type=F32)
    low_u = low_u.astype(jnp.bfloat16)
    low_h = low_h.astype(jnp.bfloat16)
    for j in range(n):
        cols = slice(j * w, (j + 1) * w)
        out_ref[j, 0:r, :] = jnp.dot(low_h, acts_ref[:, cols], preferred_element_type=F32).astype(jnp.bfloat16)
        out_ref[j, r:r2, :] = jnp.dot(low_u, cot_ref[:, cols], preferred_element_type=F32).astype(jnp.bfloat16)
        gx_ref[:, cols] = lax.dot_general(
            low_h, fac_ref[j, 0:r, :], (((0,), (0,)), ((), ())), preferred_element_type=F32
        ).astype(jnp.bfloat16)


def grads(acts, cot, factors):
    return pl.pallas_call(
        grads_kernel,
        out_shape=(
            jax.ShapeDtypeStruct(acts.shape, acts.dtype),
            jax.ShapeDtypeStruct(factors.shape, factors.dtype),
        ),
        compiler_params=pltpu.CompilerParams(vmem_limit_bytes=VMEM_LIMIT),
    )(acts, cot, factors)


def shards(acts, cotangent, down, up, adapter_per_tile, adapter_storage_slot):
    n = lax.axis_size("fsdp")
    swap = functools.partial(
        lax.all_to_all, axis_name="fsdp", split_axis=0, concat_axis=0, tiled=True
    )
    tile_adapter = lax.all_gather(adapter_per_tile, "fsdp", axis=0, tiled=True)
    labels = jnp.arange(n, dtype=jnp.int32)
    tile_slot = jnp.sum(
        jnp.where(tile_adapter[:, None] == labels[None, :], adapter_storage_slot[None, :], 0),
        axis=1,
    )
    slot_tile = jnp.sum(
        jnp.where(tile_slot[None, :] == labels[:, None], labels[None, :], 0), axis=1
    )
    spread = swap(pack(down, up, n))
    factors = swap(permute(tile_slot, spread))
    grad_x, parts = grads(acts, cotangent, factors)
    owned = swap(permute(slot_tile, swap(parts)))
    grad_a, grad_b = unpack(owned)
    return grad_x, grad_a, grad_b


def solution(mesh):
    placed = (
        P(("group", "fsdp"), None),
        P(("group", "fsdp"), None),
        P("fsdp", None, None),
        P("fsdp", None, None),
        P(("group", "fsdp")),
        P(),
    )
    return jax.shard_map(
        shards,
        mesh=mesh,
        in_specs=placed,
        out_specs=(
            P(("group", "fsdp"), None),
            P(("group", "fsdp"), None, None),
            P(("group", "fsdp"), None, None),
        ),
        check_vma=False,
    )
```

```python
import functools

import jax
import jax.numpy as jnp
from jax import lax
from jax.experimental import pallas as pl
from jax.experimental.pallas import tpu as pltpu
from jax.sharding import PartitionSpec as P

F32 = jnp.float32
BF16 = jnp.bfloat16
LANES = 128
ID_ROWS = 16
VMEM = pl.BlockSpec(memory_space=pltpu.VMEM)
SMEM = pl.BlockSpec(memory_space=pltpu.SMEM)
PARAMS = pltpu.CompilerParams(vmem_limit_bytes=48 * 1024 * 1024)


def position():
    me = lax.axis_index("fsdp")
    return me // 2, me % 2


def columns(chunk, w):
    return pl.ds(pl.multiple_of(chunk * w, w), w)


def pack_kernel(m, id_ref, down_ref, up_ref, *outs):
    p, _ = position()
    r, w = down_ref.shape[1], down_ref.shape[2] // m
    mark = jnp.full((ID_ROWS, LANES), id_ref[0].astype(F32), F32).astype(BF16)
    for k in range(m):
        for b in range(w // LANES):
            cols = pl.ds(pl.multiple_of((p ^ k) * w + b * LANES, LANES), LANES)
            outs[k][2 * r * b : 2 * r * b + r, :] = down_ref[0, :, cols]
            outs[k][2 * r * b + r : 2 * r * (b + 1), :] = up_ref[0, :, cols]
        outs[k][2 * r * (w // LANES) :, :] = mark


def stack_kernel(*refs):
    out_ref = refs[-1]
    for k, ref in enumerate(refs[:-1]):
        out_ref[k] = ref[...]


def stack(blocks):
    return pl.pallas_call(
        stack_kernel,
        out_shape=jax.ShapeDtypeStruct((len(blocks), *blocks[0].shape), BF16),
        in_specs=[VMEM] * len(blocks),
        out_specs=VMEM,
        compiler_params=PARAMS,
    )(*blocks)


def deliver_kernel(m, storage_ref, own_ref, other_ref, *outs):
    slots_ref = outs[m]
    p, c = position()
    rows = own_ref.shape[1] - ID_ROWS
    r2 = outs[0].shape[0]

    def slot_of(ref, k):
        label = jnp.max(ref[k, rows:, :].astype(F32)).astype(jnp.int32)
        return storage_ref[label]

    def copy(ref, at, out):
        for b in range(rows // r2):
            out[:, b * LANES : (b + 1) * LANES] = ref[at, b * r2 : (b + 1) * r2, :]

    for k in range(m):
        slot = slot_of(own_ref, k)
        slots_ref[2 * (p ^ k) + c] = slot
        slots_ref[2 * (p ^ k) + 1 - c] = slot_of(other_ref, k)
        at = (slot // 2) ^ p

        @pl.when(slot % 2 == c)
        def _():
            copy(own_ref, at, outs[k])

        @pl.when(slot % 2 != c)
        def _():
            copy(other_ref, at, outs[k])


def grads_kernel(m, acts_ref, cot_ref, *refs):
    factors, gx_ref, outs = refs[:m], refs[m], refs[m + 1 :]
    p, _ = position()
    r2, w = factors[0].shape
    r = r2 // 2
    rows = acts_ref.shape[0]
    dims_nt = (((1,), (1,)), ((), ()))
    low_u = jnp.zeros((r, rows), F32)
    low_h = jnp.zeros((r, rows), F32)
    for k in range(m):
        cols = columns(p ^ k, w)
        low_u += lax.dot_general(factors[k][0:r, :], acts_ref[:, cols], dims_nt, preferred_element_type=F32)
        low_h += lax.dot_general(factors[k][r:r2, :], cot_ref[:, cols], dims_nt, preferred_element_type=F32)
    low_u = low_u.astype(BF16)
    low_h = low_h.astype(BF16)
    for k in range(m):
        cols = columns(p ^ k, w)
        outs[k][0:r, :] = jnp.dot(low_h, acts_ref[:, cols], preferred_element_type=F32).astype(BF16)
        outs[k][r:r2, :] = jnp.dot(low_u, cot_ref[:, cols], preferred_element_type=F32).astype(BF16)
        gx_ref[:, cols] = lax.dot_general(
            low_h, factors[k][0:r, :], (((0,), (0,)), ((), ())), preferred_element_type=F32
        ).astype(BF16)


def collect_kernel(m, slots_ref, own_ref, other_ref, *refs):
    outs, tile_of = refs[:m], refs[m]
    p, c = position()
    for t in range(2 * m):
        tile_of[slots_ref[t]] = t
    for k in range(m):
        tile = tile_of[2 * (p ^ k) + c]
        at = (tile // 2) ^ p

        @pl.when(tile % 2 == c)
        def _():
            outs[k][...] = own_ref[at]

        @pl.when(tile % 2 != c)
        def _():
            outs[k][...] = other_ref[at]


def unpack_kernel(m, *refs):
    ga_ref, gb_ref = refs[m:]
    p, _ = position()
    r2, w = refs[0].shape
    for k in range(m):
        cols = columns(p ^ k, w)
        ga_ref[0, :, cols] = refs[k][0 : r2 // 2, :]
        gb_ref[0, :, cols] = refs[k][r2 // 2 : r2, :]


def shards(acts, cotangent, down, up, adapter_per_tile, adapter_storage_slot):
    n = lax.axis_size("fsdp")
    m = n // 2
    _, r, d = down.shape
    w = d // m

    def exchange(blocks):
        return [blocks[0]] + [
            lax.ppermute(
                blocks[k], "fsdp", [(2 * p + c, 2 * (p ^ k) + c) for p in range(m) for c in range(2)]
            )
            for k in range(1, m)
        ]

    def to_other_core(block):
        return lax.ppermute(block, "fsdp", [(f, f ^ 1) for f in range(n)])

    rows = 2 * r * w // LANES
    flat = jax.ShapeDtypeStruct((rows + ID_ROWS, LANES), BF16)
    wide = jax.ShapeDtypeStruct((2 * r, w), BF16)
    spread = pl.pallas_call(
        functools.partial(pack_kernel, m),
        out_shape=[flat] * m,
        in_specs=[SMEM, VMEM, VMEM],
        out_specs=[VMEM] * m,
        compiler_params=PARAMS,
    )(adapter_per_tile, down, up)
    held = stack(exchange(spread))
    *factors, slots = pl.pallas_call(
        functools.partial(deliver_kernel, m),
        out_shape=[wide] * m + [jax.ShapeDtypeStruct((n,), jnp.int32)],
        in_specs=[SMEM, VMEM, VMEM],
        out_specs=[VMEM] * m + [SMEM],
        compiler_params=PARAMS,
    )(adapter_storage_slot, held, to_other_core(held))
    factors = exchange(factors)
    grad_x, *parts = pl.pallas_call(
        functools.partial(grads_kernel, m),
        out_shape=[jax.ShapeDtypeStruct(acts.shape, BF16)] + [wide] * m,
        in_specs=[VMEM] * (m + 2),
        out_specs=[VMEM] * (m + 1),
        compiler_params=PARAMS,
    )(acts, cotangent, *factors)
    held = stack(exchange(parts))
    owned = pl.pallas_call(
        functools.partial(collect_kernel, m),
        out_shape=[wide] * m,
        in_specs=[SMEM, VMEM, VMEM],
        out_specs=[VMEM] * m,
        scratch_shapes=[pltpu.SMEM((n,), jnp.int32)],
        compiler_params=PARAMS,
    )(slots, held, to_other_core(held))
    grad_a, grad_b = pl.pallas_call(
        functools.partial(unpack_kernel, m),
        out_shape=[jax.ShapeDtypeStruct(down.shape, BF16)] * 2,
        in_specs=[VMEM] * m,
        out_specs=[VMEM] * 2,
        compiler_params=PARAMS,
    )(*exchange(owned))
    return grad_x, grad_a, grad_b


def solution(mesh):
    placed = (
        P(("group", "fsdp"), None),
        P(("group", "fsdp"), None),
        P("fsdp", None, None),
        P("fsdp", None, None),
        P(("group", "fsdp")),
        P(),
    )
    return jax.shard_map(
        shards,
        mesh=mesh,
        in_specs=placed,
        out_specs=(
            P(("group", "fsdp"), None),
            P(("group", "fsdp"), None, None),
            P(("group", "fsdp"), None, None),
        ),
        check_vma=False,
    )
```

```python
import functools

import jax
import jax.numpy as jnp
from jax import lax
from jax.experimental import pallas as pl
from jax.experimental.pallas import tpu as pltpu
from jax.sharding import PartitionSpec as P

F32 = jnp.float32
BF16 = jnp.bfloat16
LANES = 128
ID_ROWS = 16
VMEM = pl.BlockSpec(memory_space=pltpu.VMEM)
HBM = pl.BlockSpec(memory_space=pltpu.HBM)
SMEM = pl.BlockSpec(memory_space=pltpu.SMEM)
PARAMS = pltpu.CompilerParams(vmem_limit_bytes=48 * 1024 * 1024)


def position():
    me = lax.axis_index("fsdp")
    return me // 2, me % 2


def offsets(m):
    return [0, *range(m - 1, 0, -1)]


def columns(chunk, w):
    return pl.ds(pl.multiple_of(chunk * w, w), w)


def pack_kernel(m, id_ref, storage_ref, down_hbm, up_hbm, *refs):
    outs, down_ref, up_ref, sems = refs[:m], *refs[m:]
    p, _ = position()
    loads = [
        pltpu.make_async_copy(down_hbm, down_ref, sems.at[0]),
        pltpu.make_async_copy(up_hbm, up_ref, sems.at[1]),
    ]
    for load in loads:
        load.start()
    for load in loads:
        load.wait()
    r, w = down_ref.shape[1], down_ref.shape[2] // m
    mark = jnp.full((ID_ROWS, LANES), storage_ref[id_ref[0]].astype(F32), F32).astype(BF16)
    for out, k in zip(outs, offsets(m)):
        for b in range(w // LANES):
            cols = pl.ds(pl.multiple_of((p ^ k) * w + b * LANES, LANES), LANES)
            out[2 * r * b : 2 * r * b + r, :] = down_ref[0, :, cols]
            out[2 * r * b + r : 2 * r * (b + 1), :] = up_ref[0, :, cols]
        out[2 * r * (w // LANES) :, :] = mark


def stack_kernel(*refs):
    *blocks, held_ref = refs
    for block, k in zip(blocks, offsets(len(blocks))):
        held_ref[k] = block[...]


def stack(blocks):
    return pl.pallas_call(
        stack_kernel,
        out_shape=jax.ShapeDtypeStruct((len(blocks), *blocks[0].shape), BF16),
        in_specs=[VMEM] * len(blocks),
        out_specs=VMEM,
        compiler_params=PARAMS,
    )(*blocks)


def slot_of(ref, k):
    return ref[k, ref.shape[1] - ID_ROWS :, :].astype(F32)[0, 0].astype(jnp.int32)


def deliver_kernel(m, own_ref, other_ref, *outs):
    p, c = position()
    r2 = outs[0].shape[0]
    blocks = (own_ref.shape[1] - ID_ROWS) // r2
    slots = [slot_of(own_ref, k) for k in offsets(m)]
    for out, slot in zip(outs, slots):
        at, here = (slot // 2) ^ p, slot % 2 == c
        for b in range(blocks):
            rows = slice(b * r2, (b + 1) * r2)
            out[:, b * LANES : (b + 1) * LANES] = jnp.where(
                here, own_ref[at, rows, :], other_ref[at, rows, :]
            )


def inverse_kernel(m, own_ref, other_ref, tile_of):
    p, c = position()
    for ref, core in ((own_ref, c), (other_ref, 1 - c)):
        slots = [slot_of(ref, k) for k in range(m)]
        for k, slot in enumerate(slots):
            tile_of[slot] = 2 * (p ^ k) + core


def grads_kernel(m, acts_ref, cot_ref, *refs):
    factors, low_ref, outs = refs[:m], refs[m], refs[m + 1 :]
    p, _ = position()
    r2, w = factors[0].shape
    r = r2 // 2
    rows = acts_ref.shape[0]
    dims_nt = (((1,), (1,)), ((), ()))
    low_u = jnp.zeros((r, rows), F32)
    low_h = jnp.zeros((r, rows), F32)
    for factor, k in zip(factors, offsets(m)):
        cols = columns(p ^ k, w)
        low_u += lax.dot_general(factor[0:r, :], acts_ref[:, cols], dims_nt, preferred_element_type=F32)
        low_h += lax.dot_general(factor[r:r2, :], cot_ref[:, cols], dims_nt, preferred_element_type=F32)
    low_u = low_u.astype(BF16)
    low_h = low_h.astype(BF16)
    low_ref[...] = low_h
    for out, k in zip(outs, offsets(m)):
        cols = columns(p ^ k, w)
        out[0:r, :] = jnp.dot(low_h, acts_ref[:, cols], preferred_element_type=F32).astype(BF16)
        out[r:r2, :] = jnp.dot(low_u, cot_ref[:, cols], preferred_element_type=F32).astype(BF16)


def inputs_kernel(m, low_ref, *refs):
    factors, gx_ref = refs[:m], refs[m]
    p, _ = position()
    r2, w = factors[0].shape
    for factor, k in zip(factors, offsets(m)):
        gx_ref[:, columns(p ^ k, w)] = lax.dot_general(
            low_ref[...], factor[0 : r2 // 2, :], (((0,), (0,)), ((), ())), preferred_element_type=F32
        ).astype(BF16)


def collect_kernel(m, tile_of, own_ref, other_ref, *outs):
    p, c = position()
    for out, k in zip(outs, offsets(m)):
        tile = tile_of[2 * (p ^ k) + c]
        at, here = (tile // 2) ^ p, tile % 2 == c
        out[...] = jnp.where(here, own_ref[at], other_ref[at])


def unpack_kernel(m, *refs):
    ga_ref, gb_ref = refs[m:]
    p, _ = position()
    r2, w = refs[0].shape
    for block, k in zip(refs, offsets(m)):
        cols = columns(p ^ k, w)
        ga_ref[0, :, cols] = block[0 : r2 // 2, :]
        gb_ref[0, :, cols] = block[r2 // 2 : r2, :]


def shards(acts, cotangent, down, up, adapter_per_tile, adapter_storage_slot):
    n = lax.axis_size("fsdp")
    m = n // 2
    _, r, d = down.shape
    w = d // m

    def exchange(blocks):
        return [blocks[0]] + [
            lax.ppermute(
                block, "fsdp", [(2 * p + c, 2 * (p ^ k) + c) for p in range(m) for c in range(2)]
            )
            for block, k in zip(blocks[1:], offsets(m)[1:])
        ]

    def to_other_core(block):
        return lax.ppermute(block, "fsdp", [(f, f ^ 1) for f in range(n)])

    rows = 2 * r * w // LANES
    flat = jax.ShapeDtypeStruct((rows + ID_ROWS, LANES), BF16)
    wide = jax.ShapeDtypeStruct((2 * r, w), BF16)
    spread = pl.pallas_call(
        functools.partial(pack_kernel, m),
        out_shape=[flat] * m,
        in_specs=[SMEM, SMEM, HBM, HBM],
        out_specs=[VMEM] * m,
        scratch_shapes=[
            pltpu.VMEM(down.shape, BF16),
            pltpu.VMEM(up.shape, BF16),
            pltpu.SemaphoreType.DMA((2,)),
        ],
        compiler_params=PARAMS,
    )(adapter_per_tile, adapter_storage_slot, down, up)
    own = stack(exchange(spread))
    other = to_other_core(own)
    factors = pl.pallas_call(
        functools.partial(deliver_kernel, m),
        out_shape=[wide] * m,
        in_specs=[VMEM, VMEM],
        out_specs=[VMEM] * m,
        compiler_params=PARAMS,
    )(own, other)
    factors = exchange(factors)
    tile_of = pl.pallas_call(
        functools.partial(inverse_kernel, m),
        out_shape=jax.ShapeDtypeStruct((n,), jnp.int32),
        in_specs=[VMEM, VMEM],
        out_specs=SMEM,
        compiler_params=PARAMS,
    )(own, other)
    low, *parts = pl.pallas_call(
        functools.partial(grads_kernel, m),
        out_shape=[jax.ShapeDtypeStruct((r, acts.shape[0]), BF16)] + [wide] * m,
        in_specs=[VMEM] * (m + 2),
        out_specs=[VMEM] * (m + 1),
        compiler_params=PARAMS,
    )(acts, cotangent, *factors)
    parts = exchange(parts)
    grad_x = pl.pallas_call(
        functools.partial(inputs_kernel, m),
        out_shape=jax.ShapeDtypeStruct(acts.shape, BF16),
        in_specs=[VMEM] * (m + 1),
        out_specs=VMEM,
        compiler_params=PARAMS,
        cost_estimate=pl.CostEstimate(
            flops=2 * r * acts.size, bytes_accessed=2 * acts.size, transcendentals=0
        ),
    )(low, *factors)
    own = stack(parts)
    owned = pl.pallas_call(
        functools.partial(collect_kernel, m),
        out_shape=[wide] * m,
        in_specs=[SMEM, VMEM, VMEM],
        out_specs=[VMEM] * m,
        compiler_params=PARAMS,
    )(tile_of, own, to_other_core(own))
    grad_a, grad_b = pl.pallas_call(
        functools.partial(unpack_kernel, m),
        out_shape=[jax.ShapeDtypeStruct(down.shape, BF16)] * 2,
        in_specs=[VMEM] * m,
        out_specs=[VMEM] * 2,
        compiler_params=PARAMS,
    )(*exchange(owned))
    return grad_x, grad_a, grad_b


def solution(mesh):
    placed = (
        P(("group", "fsdp"), None),
        P(("group", "fsdp"), None),
        P("fsdp", None, None),
        P("fsdp", None, None),
        P(("group", "fsdp")),
        P(),
    )
    return jax.shard_map(
        shards,
        mesh=mesh,
        in_specs=placed,
        out_specs=(
            P(("group", "fsdp"), None),
            P(("group", "fsdp"), None, None),
            P(("group", "fsdp"), None, None),
        ),
        check_vma=False,
    )
```

```python
import jax
import jax.numpy as jnp
from jax import lax
from jax.experimental import pallas as pl
from jax.experimental.pallas import tpu as pltpu
from jax.sharding import PartitionSpec as P

F32 = jnp.float32
BF16 = jnp.bfloat16
LANES = 128
ID_ROWS = 16
VMEM = pl.BlockSpec(memory_space=pltpu.VMEM)
HBM = pl.BlockSpec(memory_space=pltpu.HBM)
SMEM = pl.BlockSpec(memory_space=pltpu.SMEM)
PARAMS = pltpu.CompilerParams(vmem_limit_bytes=48 * 1024 * 1024)


def position():
    me = lax.axis_index("fsdp")
    return me // 2, me % 2


def pack_kernel(id_ref, storage_ref, down_hbm, up_hbm, out_ref, down_ref, up_ref, sems):
    m = out_ref.shape[0]
    loads = [
        pltpu.make_async_copy(down_hbm, down_ref, sems.at[0]),
        pltpu.make_async_copy(up_hbm, up_ref, sems.at[1]),
    ]
    for load in loads:
        load.start()
    for load in loads:
        load.wait()
    r, blocks = down_ref.shape[1], down_ref.shape[2] // m // LANES
    mark = jnp.full((ID_ROWS, LANES), storage_ref[id_ref[0]].astype(F32), F32).astype(BF16)
    for j in range(m):
        for b in range(blocks):
            cols = slice((j * blocks + b) * LANES, (j * blocks + b + 1) * LANES)
            out_ref[j, 2 * r * b : 2 * r * b + r, :] = down_ref[0, :, cols]
            out_ref[j, 2 * r * b + r : 2 * r * (b + 1), :] = up_ref[0, :, cols]
        out_ref[j, 2 * r * blocks :, :] = mark


def slot_of(ref, j):
    return ref[j, ref.shape[1] - ID_ROWS :, :].astype(F32)[0, 0].astype(jnp.int32)


def deliver_kernel(own_ref, other_ref, out_ref):
    _, c = position()
    m, r2, _ = out_ref.shape
    blocks = (own_ref.shape[1] - ID_ROWS) // r2
    slots = [slot_of(own_ref, j) for j in range(m)]
    for j, slot in enumerate(slots):
        at, here = slot // 2, slot % 2 == c
        for b in range(blocks):
            rows = slice(b * r2, (b + 1) * r2)
            out_ref[j, :, b * LANES : (b + 1) * LANES] = jnp.where(
                here, own_ref[at, rows, :], other_ref[at, rows, :]
            )


def inverse_kernel(own_ref, other_ref, tile_of):
    _, c = position()
    m = own_ref.shape[0]
    for ref, core in ((own_ref, c), (other_ref, 1 - c)):
        slots = [slot_of(ref, j) for j in range(m)]
        for j, slot in enumerate(slots):
            tile_of[slot] = 2 * j + core


def grads_kernel(acts_ref, cot_ref, factors_ref, low_ref, out_ref):
    m, r2, w = factors_ref.shape
    r = r2 // 2
    rows = acts_ref.shape[0]
    dims_nt = (((1,), (1,)), ((), ()))
    low_u = jnp.zeros((r, rows), F32)
    low_h = jnp.zeros((r, rows), F32)
    for j in range(m):
        cols = slice(j * w, (j + 1) * w)
        low_u += lax.dot_general(factors_ref[j, 0:r, :], acts_ref[:, cols], dims_nt, preferred_element_type=F32)
        low_h += lax.dot_general(factors_ref[j, r:r2, :], cot_ref[:, cols], dims_nt, preferred_element_type=F32)
    low_u = low_u.astype(BF16)
    low_h = low_h.astype(BF16)
    low_ref[...] = low_h
    for j in range(m):
        cols = slice(j * w, (j + 1) * w)
        out_ref[j, 0:r, :] = jnp.dot(low_h, acts_ref[:, cols], preferred_element_type=F32).astype(BF16)
        out_ref[j, r:r2, :] = jnp.dot(low_u, cot_ref[:, cols], preferred_element_type=F32).astype(BF16)


def inputs_kernel(low_ref, factors_ref, gx_ref):
    m, r2, w = factors_ref.shape
    for j in range(m):
        gx_ref[:, j * w : (j + 1) * w] = lax.dot_general(
            low_ref[...], factors_ref[j, 0 : r2 // 2, :], (((0,), (0,)), ((), ())), preferred_element_type=F32
        ).astype(BF16)


def collect_kernel(tile_of, own_ref, other_ref, out_ref):
    _, c = position()
    for j in range(out_ref.shape[0]):
        tile = tile_of[2 * j + c]
        out_ref[j] = jnp.where(tile % 2 == c, own_ref[tile // 2], other_ref[tile // 2])


def unpack_kernel(in_ref, ga_ref, gb_ref):
    m, r2, w = in_ref.shape
    for j in range(m):
        ga_ref[0, :, j * w : (j + 1) * w] = in_ref[j, 0 : r2 // 2, :]
        gb_ref[0, :, j * w : (j + 1) * w] = in_ref[j, r2 // 2 : r2, :]


def call(kernel, out_shape, in_specs, out_specs, **options):
    return pl.pallas_call(
        kernel,
        out_shape=out_shape,
        in_specs=in_specs,
        out_specs=out_specs,
        compiler_params=PARAMS,
        **options,
    )


def shards(acts, cotangent, down, up, adapter_per_tile, adapter_storage_slot):
    n = lax.axis_size("fsdp")
    m = n // 2
    _, r, d = down.shape
    w = d // m
    cores = [[2 * p + c for p in range(m)] for c in range(2)]

    def exchange(blocks):
        return lax.all_to_all(
            blocks, "fsdp", split_axis=0, concat_axis=0, tiled=True, axis_index_groups=cores
        )

    def to_other_core(block):
        return lax.ppermute(block, "fsdp", [(f, f ^ 1) for f in range(n)])

    flat = jax.ShapeDtypeStruct((m, 2 * r * w // LANES + ID_ROWS, LANES), BF16)
    wide = jax.ShapeDtypeStruct((m, 2 * r, w), BF16)
    low = jax.ShapeDtypeStruct((r, acts.shape[0]), BF16)
    own = exchange(
        call(
            pack_kernel,
            flat,
            [SMEM, SMEM, HBM, HBM],
            VMEM,
            scratch_shapes=[
                pltpu.VMEM(down.shape, BF16),
                pltpu.VMEM(up.shape, BF16),
                pltpu.SemaphoreType.DMA((2,)),
            ],
        )(adapter_per_tile, adapter_storage_slot, down, up)
    )
    other = to_other_core(own)
    factors = exchange(call(deliver_kernel, wide, [VMEM] * 2, VMEM)(own, other))
    tile_of = call(inverse_kernel, jax.ShapeDtypeStruct((n,), jnp.int32), [VMEM] * 2, SMEM)(own, other)
    low, parts = call(grads_kernel, (low, wide), [VMEM] * 3, [VMEM] * 2)(acts, cotangent, factors)
    own = exchange(parts)
    grad_x = call(
        inputs_kernel,
        jax.ShapeDtypeStruct(acts.shape, BF16),
        [VMEM] * 2,
        VMEM,
        cost_estimate=pl.CostEstimate(
            flops=2 * r * acts.size, bytes_accessed=2 * acts.size, transcendentals=0
        ),
    )(low, factors)
    owned = call(collect_kernel, wide, [SMEM, VMEM, VMEM], VMEM)(tile_of, own, to_other_core(own))
    grad_a, grad_b = call(
        unpack_kernel, [jax.ShapeDtypeStruct(down.shape, BF16)] * 2, [VMEM], [VMEM] * 2
    )(exchange(owned))
    return grad_x, grad_a, grad_b


def solution(mesh):
    placed = (
        P(("group", "fsdp"), None),
        P(("group", "fsdp"), None),
        P("fsdp", None, None),
        P("fsdp", None, None),
        P(("group", "fsdp")),
        P(),
    )
    return jax.shard_map(
        shards,
        mesh=mesh,
        in_specs=placed,
        out_specs=(
            P(("group", "fsdp"), None),
            P(("group", "fsdp"), None, None),
            P(("group", "fsdp"), None, None),
        ),
        check_vma=False,
    )
```

```python
import functools

import jax
import jax.numpy as jnp
from jax import lax
from jax.experimental import pallas as pl
from jax.experimental.pallas import tpu as pltpu
from jax.sharding import PartitionSpec as P

F32 = jnp.float32
BF16 = jnp.bfloat16
LANES = 128
ID_ROWS = 16
VMEM = pl.BlockSpec(memory_space=pltpu.VMEM)
HBM = pl.BlockSpec(memory_space=pltpu.HBM)
SMEM = pl.BlockSpec(memory_space=pltpu.SMEM)
PARAMS = pltpu.CompilerParams(vmem_limit_bytes=32 * 1024 * 1024)
ALONE = pltpu.CompilerParams(vmem_limit_bytes=60 * 1024 * 1024)


def position():
    me = lax.axis_index("fsdp")
    return me // 2, me % 2


def halves(m):
    return [*range(m // 2)], [*range(m - 1, m // 2 - 1, -1)]


def offsets(m):
    near, far = halves(m)
    return near[:1] + far[:2] + near[1:2] + far[2:] + near[2:]


def columns(chunk, w):
    return pl.ds(pl.multiple_of(chunk * w, w), w)


def pack_kernel(m, id_ref, storage_ref, down_hbm, up_hbm, *refs):
    outs, down_ref, up_ref, sems = refs[:m], *refs[m:]
    p, _ = position()
    loads = [
        pltpu.make_async_copy(down_hbm, down_ref, sems.at[0]),
        pltpu.make_async_copy(up_hbm, up_ref, sems.at[1]),
    ]
    for load in loads:
        load.start()
    for load in loads:
        load.wait()
    r, w = down_ref.shape[1], down_ref.shape[2] // m
    mark = jnp.full((ID_ROWS, LANES), storage_ref[id_ref[0]].astype(F32), F32).astype(BF16)
    for out, k in zip(outs, offsets(m)):
        for b in range(w // LANES):
            cols = pl.ds(pl.multiple_of((p ^ k) * w + b * LANES, LANES), LANES)
            out[2 * r * b : 2 * r * b + r, :] = down_ref[0, :, cols]
            out[2 * r * b + r : 2 * r * (b + 1), :] = up_ref[0, :, cols]
        out[2 * r * (w // LANES) :, :] = mark


def stack_kernel(*refs):
    *blocks, held_ref = refs
    for at, block in enumerate(blocks):
        held_ref[at] = block[...]


def stack(blocks):
    return pl.pallas_call(
        stack_kernel,
        out_shape=jax.ShapeDtypeStruct((len(blocks), *blocks[0].shape), BF16),
        in_specs=[VMEM] * len(blocks),
        out_specs=VMEM,
        compiler_params=PARAMS,
    )(*blocks)


def pick(held, chip, here, rows):
    own_near, own_far, other_near, other_far = held
    h = own_near.shape[0]
    k = chip ^ position()[0]
    near, u, v = k < h, lax.rem(k, h), h - 1 - lax.rem(k, h)
    own = jnp.where(near, own_near[u, rows, :], own_far[v, rows, :])
    other = jnp.where(near, other_near[u, rows, :], other_far[v, rows, :])
    return jnp.where(here, own, other)


def slot_of(near, far, k):
    h = near.shape[0]
    ref, at = (near, k) if k < h else (far, 2 * h - 1 - k)
    return ref[at, ref.shape[1] - ID_ROWS :, :].astype(F32)[0, 0].astype(jnp.int32)


def deliver_kernel(m, *refs):
    held, outs = refs[:4], refs[4:]
    _, c = position()
    r2 = outs[0].shape[0]
    blocks = (held[0].shape[1] - ID_ROWS) // r2
    slots = [slot_of(*held[:2], k) for k in offsets(m)]
    for out, slot in zip(outs, slots):
        for b in range(blocks):
            rows = slice(b * r2, (b + 1) * r2)
            out[:, b * LANES : (b + 1) * LANES] = pick(held, slot // 2, slot % 2 == c, rows)


def inverse_kernel(m, own_near, own_far, other_near, other_far, tile_of):
    p, c = position()
    for near, far, core in ((own_near, own_far, c), (other_near, other_far, 1 - c)):
        slots = [slot_of(near, far, k) for k in range(m)]
        for k, slot in enumerate(slots):
            tile_of[slot] = 2 * (p ^ k) + core


def touch_kernel(_, token_ref):
    token_ref[...] = jnp.zeros_like(token_ref)


def grads_kernel(m, _, acts_ref, cot_ref, *refs):
    factors, low_ref, outs = refs[:m], refs[m], refs[m + 1 :]
    p, _ = position()
    r2, w = factors[0].shape
    r = r2 // 2
    rows = acts_ref.shape[0]
    dims_nt = (((1,), (1,)), ((), ()))
    low_u = jnp.zeros((r, rows), F32)
    low_h = jnp.zeros((r, rows), F32)
    for factor, k in zip(factors, offsets(m)):
        cols = columns(p ^ k, w)
        low_u += lax.dot_general(factor[0:r, :], acts_ref[:, cols], dims_nt, preferred_element_type=F32)
        low_h += lax.dot_general(factor[r:r2, :], cot_ref[:, cols], dims_nt, preferred_element_type=F32)
    low_u = low_u.astype(BF16)
    low_h = low_h.astype(BF16)
    low_ref[...] = low_h
    for out, k in zip(outs, offsets(m)):
        cols = columns(p ^ k, w)
        out[0:r, :] = jnp.dot(low_h, acts_ref[:, cols], preferred_element_type=F32).astype(BF16)
        out[r:r2, :] = jnp.dot(low_u, cot_ref[:, cols], preferred_element_type=F32).astype(BF16)


def inputs_kernel(m, low_ref, *refs):
    factors, gx_ref = refs[:m], refs[m]
    p, _ = position()
    r2, w = factors[0].shape
    for factor, k in zip(factors, offsets(m)):
        gx_ref[:, columns(p ^ k, w)] = lax.dot_general(
            low_ref[...], factor[0 : r2 // 2, :], (((0,), (0,)), ((), ())), preferred_element_type=F32
        ).astype(BF16)


def collect_kernel(m, tile_of, *refs):
    held, outs = refs[:4], refs[4:]
    p, c = position()
    for out, k in zip(outs, offsets(m)):
        tile = tile_of[2 * (p ^ k) + c]
        out[...] = pick(held, tile // 2, tile % 2 == c, slice(None))


def unpack_kernel(m, *refs):
    ga_ref, gb_ref = refs[m:]
    p, _ = position()
    r2, w = refs[0].shape
    for block, k in zip(refs, offsets(m)):
        cols = columns(p ^ k, w)
        ga_ref[0, :, cols] = block[0 : r2 // 2, :]
        gb_ref[0, :, cols] = block[r2 // 2 : r2, :]


def shards(acts, cotangent, down, up, adapter_per_tile, adapter_storage_slot):
    n = lax.axis_size("fsdp")
    m = n // 2
    _, r, d = down.shape
    w = d // m

    def exchange(blocks):
        return [blocks[0]] + [
            lax.ppermute(
                block, "fsdp", [(2 * p + c, 2 * (p ^ k) + c) for p in range(m) for c in range(2)]
            )
            for block, k in zip(blocks[1:], offsets(m)[1:])
        ]

    def gather(blocks):
        by_offset = dict(zip(offsets(m), blocks))
        own = [stack([by_offset[k] for k in half]) for half in halves(m)]
        return own + [lax.ppermute(half, "fsdp", [(f, f ^ 1) for f in range(n)]) for half in own]

    rows = 2 * r * w // LANES
    flat = jax.ShapeDtypeStruct((rows + ID_ROWS, LANES), BF16)
    wide = jax.ShapeDtypeStruct((2 * r, w), BF16)
    spread = pl.pallas_call(
        functools.partial(pack_kernel, m),
        out_shape=[flat] * m,
        in_specs=[SMEM, SMEM, HBM, HBM],
        out_specs=[VMEM] * m,
        scratch_shapes=[
            pltpu.VMEM(down.shape, BF16),
            pltpu.VMEM(up.shape, BF16),
            pltpu.SemaphoreType.DMA((2,)),
        ],
        compiler_params=ALONE,
    )(adapter_per_tile, adapter_storage_slot, down, up)
    token = pl.pallas_call(
        touch_kernel,
        out_shape=jax.ShapeDtypeStruct((8, LANES), F32),
        in_specs=[VMEM],
        out_specs=VMEM,
        compiler_params=PARAMS,
    )(cotangent)
    first = stack(spread[:1])[0]
    held = gather(exchange([first, *spread[1:]]))
    factors = pl.pallas_call(
        functools.partial(deliver_kernel, m),
        out_shape=[wide] * m,
        in_specs=[VMEM] * 4,
        out_specs=[VMEM] * m,
        compiler_params=PARAMS,
    )(*held)
    factors = exchange(factors)
    tile_of = pl.pallas_call(
        functools.partial(inverse_kernel, m),
        out_shape=jax.ShapeDtypeStruct((n,), jnp.int32),
        in_specs=[VMEM] * 4,
        out_specs=SMEM,
        compiler_params=PARAMS,
    )(*held)
    low, *parts = pl.pallas_call(
        functools.partial(grads_kernel, m),
        out_shape=[jax.ShapeDtypeStruct((r, acts.shape[0]), BF16)] + [wide] * m,
        in_specs=[VMEM] * (m + 3),
        out_specs=[VMEM] * (m + 1),
        compiler_params=PARAMS,
    )(token, acts, cotangent, *factors)
    parts = exchange(parts)
    grad_x = pl.pallas_call(
        functools.partial(inputs_kernel, m),
        out_shape=jax.ShapeDtypeStruct(acts.shape, BF16),
        in_specs=[VMEM] * (m + 1),
        out_specs=VMEM,
        compiler_params=PARAMS,
        cost_estimate=pl.CostEstimate(
            flops=2 * r * acts.size, bytes_accessed=2 * acts.size, transcendentals=0
        ),
    )(low, *factors)
    owned = pl.pallas_call(
        functools.partial(collect_kernel, m),
        out_shape=[wide] * m,
        in_specs=[SMEM] + [VMEM] * 4,
        out_specs=[VMEM] * m,
        compiler_params=PARAMS,
    )(tile_of, *gather(parts))
    grad_a, grad_b = pl.pallas_call(
        functools.partial(unpack_kernel, m),
        out_shape=[jax.ShapeDtypeStruct(down.shape, BF16)] * 2,
        in_specs=[VMEM] * m,
        out_specs=[VMEM] * 2,
        compiler_params=PARAMS,
    )(*exchange(owned))
    return grad_x, grad_a, grad_b


def solution(mesh):
    placed = (
        P(("group", "fsdp"), None),
        P(("group", "fsdp"), None),
        P("fsdp", None, None),
        P("fsdp", None, None),
        P(("group", "fsdp")),
        P(),
    )
    return jax.shard_map(
        shards,
        mesh=mesh,
        in_specs=placed,
        out_specs=(
            P(("group", "fsdp"), None),
            P(("group", "fsdp"), None, None),
            P(("group", "fsdp"), None, None),
        ),
        check_vma=False,
    )
```

```python
import functools

import jax
import jax.numpy as jnp
from jax import lax
from jax.experimental import pallas as pl
from jax.experimental.pallas import tpu as pltpu
from jax.sharding import PartitionSpec as P

F32 = jnp.float32
BF16 = jnp.bfloat16
LANES = 128
ID_ROWS = 16
VMEM = pl.BlockSpec(memory_space=pltpu.VMEM)
HBM = pl.BlockSpec(memory_space=pltpu.HBM)
SMEM = pl.BlockSpec(memory_space=pltpu.SMEM)
PARAMS = pltpu.CompilerParams(vmem_limit_bytes=32 * 1024 * 1024)
ALONE = pltpu.CompilerParams(vmem_limit_bytes=60 * 1024 * 1024)


def position():
    me = lax.axis_index("fsdp")
    return me // 2, me % 2


def far_offsets(m):
    return range(m - 1, m // 2 - 1, -1)


def chips(m):
    p, _ = position()
    h = m // 2
    return [p // h * h + q for q in range(h)] + [p ^ k for k in far_offsets(m)]


def blocks(near, far):
    return [near.at[q] for q in range(near.shape[0])] + list(far)


def columns(chip, w, first=0, size=None):
    size = size or w
    return pl.ds(pl.multiple_of(chip * w + first, LANES), size)


def pack_kernel(m, id_ref, storage_ref, down_hbm, up_hbm, near_hbm, *refs):
    far_hbm, (down_ref, up_ref, out_ref, load_sems, store_sems) = refs[: m // 2], refs[m // 2 :]
    r, w = down_ref.shape[0], down_ref.shape[1] // m
    order = [*zip(range(m), chips(m), blocks(near_hbm, far_hbm))]
    order = order[m // 2 :] + order[: m // 2]
    loads = []
    for i, chip, _ in order:
        cols = columns(chip, w)
        loads.append(
            [
                pltpu.make_async_copy(src.at[0, :, cols], dst.at[:, i * w : (i + 1) * w], sem)
                for src, dst, sem in (
                    (down_hbm, down_ref, load_sems.at[0, i]),
                    (up_hbm, up_ref, load_sems.at[1, i]),
                )
            ]
        )
        for load in loads[-1]:
            load.start()
    mark = jnp.full((ID_ROWS, LANES), storage_ref[id_ref[0]].astype(F32), F32).astype(BF16)
    stores = []
    for (i, _, dst), pair in zip(order, loads):
        for load in pair:
            load.wait()
        for b in range(w // LANES):
            cols = slice(i * w + b * LANES, i * w + (b + 1) * LANES)
            out_ref[i, 2 * r * b : 2 * r * b + r, :] = down_ref[:, cols]
            out_ref[i, 2 * r * b + r : 2 * r * (b + 1), :] = up_ref[:, cols]
        out_ref[i, 2 * r * (w // LANES) :, :] = mark
        stores.append(pltpu.make_async_copy(out_ref.at[i], dst, store_sems.at[i]))
        stores[-1].start()
    for store in stores:
        store.wait()


def stack_kernel(*refs):
    *parts, out_ref = refs
    for i, part in enumerate(parts):
        out_ref[i] = part[...]


def slot_of(block):
    mark = block[block.shape[0] - ID_ROWS :, :]
    return mark.astype(F32)[0, 0].astype(jnp.int32)


def pick(held, chip, here, rows, cols):
    own_near, own_far, other_near, other_far = held
    h = own_near.shape[0]
    p, _ = position()
    is_near, u, v = chip // h == p // h, chip % h, 2 * h - 1 - (chip ^ p)
    u, v = jnp.where(is_near, u, 0), jnp.where(is_near, 0, v)
    own = jnp.where(is_near, own_near[u, rows, cols], own_far[v, rows, cols])
    other = jnp.where(is_near, other_near[u, rows, cols], other_far[v, rows, cols])
    return jnp.where(here, own, other)


def deliver_kernel(m, own_near, own_far, other_near, other_far, near_ref, *far):
    _, c = position()
    outs = blocks(near_ref, far)
    r2, w = outs[0].shape
    slots = [slot_of(block) for block in blocks(own_near, blocks(own_far, ()))]
    for out, slot in zip(outs, slots):
        for b in range(w // LANES):
            out[:, b * LANES : (b + 1) * LANES] = pick(
                (own_near, own_far, other_near, other_far),
                slot // 2,
                slot % 2 == c,
                slice(b * r2, (b + 1) * r2),
                slice(None),
            )


def inverse_kernel(m, own_near, own_far, other_near, other_far, tile_of):
    _, c = position()
    for near, far, core in ((own_near, own_far, c), (other_near, other_far, 1 - c)):
        slots = [slot_of(block) for block in blocks(near, blocks(far, ()))]
        for chip, slot in zip(chips(m), slots):
            tile_of[slot] = 2 * chip + core


def touch_kernel(after, array, token_ref):
    token_ref[...] = jnp.zeros_like(token_ref)


def grads_kernel(m, _, acts_ref, cot_ref, near_in, *refs):
    far_in, low_ref, near_out, far_out = refs[: m // 2], refs[m // 2], refs[m // 2 + 1], refs[m // 2 + 2 :]
    r2, w = near_in.shape[1:]
    r = r2 // 2
    rows = acts_ref.shape[0]
    dims_nt = (((1,), (1,)), ((), ()))
    low_u = jnp.zeros((r, rows), F32)
    low_h = jnp.zeros((r, rows), F32)
    for chip, factor in zip(chips(m), blocks(near_in, far_in)):
        cols = columns(chip, w)
        low_u += lax.dot_general(factor[0:r, :], acts_ref[:, cols], dims_nt, preferred_element_type=F32)
        low_h += lax.dot_general(factor[r:r2, :], cot_ref[:, cols], dims_nt, preferred_element_type=F32)
    low_u = low_u.astype(BF16)
    low_h = low_h.astype(BF16)
    low_ref[...] = low_h
    for chip, out in zip(chips(m), blocks(near_out, far_out)):
        cols = columns(chip, w)
        out[0:r, :] = jnp.dot(low_h, acts_ref[:, cols], preferred_element_type=F32).astype(BF16)
        out[r:r2, :] = jnp.dot(low_u, cot_ref[:, cols], preferred_element_type=F32).astype(BF16)


def inputs_kernel(m, _, low_ref, near_ref, *refs):
    far, gx_ref = refs[: m // 2], refs[m // 2]
    r2, w = near_ref.shape[1:]
    for chip, factor in zip(chips(m), blocks(near_ref, far)):
        gx_ref[:, columns(chip, w)] = lax.dot_general(
            low_ref[...], factor[0 : r2 // 2, :], (((0,), (0,)), ((), ())), preferred_element_type=F32
        ).astype(BF16)


def collect_kernel(m, tile_of, own_near, own_far, other_near, other_far, near_ref, *far):
    _, c = position()
    w = near_ref.shape[2]
    for chip, out in zip(chips(m), blocks(near_ref, far)):
        tile = tile_of[2 * chip + c]
        for b in range(w // LANES):
            cols = slice(b * LANES, (b + 1) * LANES)
            out[:, cols] = pick(
                (own_near, own_far, other_near, other_far), tile // 2, tile % 2 == c, slice(None), cols
            )


def unpack_kernel(m, near_ref, *refs):
    far, (ga_hbm, gb_hbm, sems) = refs[: m // 2], refs[m // 2 :]
    r2, w = near_ref.shape[1:]
    stores = []
    for i, (chip, block) in enumerate(zip(chips(m), blocks(near_ref, far))):
        for j, out in enumerate((ga_hbm, gb_hbm)):
            rows = pl.ds(j * (r2 // 2), r2 // 2)
            stores.append(
                pltpu.make_async_copy(block.at[rows, :], out.at[0, :, columns(chip, w)], sems.at[j, i])
            )
            stores[-1].start()
    for store in stores:
        store.wait()


def call(kernel, out_shape, in_specs, out_specs, params=PARAMS, **options):
    return pl.pallas_call(
        kernel,
        out_shape=out_shape,
        in_specs=in_specs,
        out_specs=out_specs,
        compiler_params=params,
        **options,
    )


def shards(acts, cotangent, down, up, adapter_per_tile, adapter_storage_slot):
    n = lax.axis_size("fsdp")
    m = n // 2
    h = m // 2
    _, r, d = down.shape
    w = d // m

    def exchange(near, *far):
        pairs = [
            [(2 * p + c, 2 * (p ^ k) + c) for p in range(m) for c in range(2)] for k in far_offsets(m)
        ]
        far = [lax.ppermute(block, "fsdp", pair) for block, pair in zip(far, pairs)]
        groups = [[2 * (s * h + q) + c for q in range(h)] for s in range(2) for c in range(2)]
        near = lax.all_to_all(
            near, "fsdp", split_axis=0, concat_axis=0, tiled=True, axis_index_groups=groups
        )
        return near, *far

    def gather(near, *far):
        stacked = jax.ShapeDtypeStruct((h, *far[0].shape), BF16)
        own = [near, call(stack_kernel, stacked, [VMEM] * h, VMEM)(*far)]
        return own + [lax.ppermute(half, "fsdp", [(f, f ^ 1) for f in range(n)]) for half in own]

    def shapes(rows, cols):
        one = jax.ShapeDtypeStruct((rows, cols), BF16)
        return [jax.ShapeDtypeStruct((h, rows, cols), BF16)] + [one] * h

    flat = shapes(2 * r * w // LANES + ID_ROWS, LANES)
    wide = shapes(2 * r, w)
    spread = call(
        functools.partial(pack_kernel, m),
        flat,
        [SMEM, SMEM, HBM, HBM],
        [HBM] * (h + 1),
        ALONE,
        scratch_shapes=[
            pltpu.VMEM((r, d), BF16),
            pltpu.VMEM((r, d), BF16),
            pltpu.VMEM((m, *flat[1].shape), BF16),
            pltpu.SemaphoreType.DMA((2, m)),
            pltpu.SemaphoreType.DMA((m,)),
        ],
    )(adapter_per_tile, adapter_storage_slot, down, up)
    held = gather(*exchange(*spread))
    factors = call(functools.partial(deliver_kernel, m), wide, [VMEM] * 4, [VMEM] * (h + 1))(*held)
    token = call(touch_kernel, jax.ShapeDtypeStruct((8, LANES), F32), [VMEM] * 2, VMEM)(
        factors[-1], cotangent
    )
    factors = exchange(*factors)
    tile_of = call(
        functools.partial(inverse_kernel, m), jax.ShapeDtypeStruct((n,), jnp.int32), [VMEM] * 4, SMEM
    )(*held)
    low, *parts = call(
        functools.partial(grads_kernel, m),
        [jax.ShapeDtypeStruct((r, acts.shape[0]), BF16)] + wide,
        [VMEM] * (h + 4),
        [VMEM] * (h + 2),
    )(token, acts, cotangent, *factors)
    parts = exchange(*parts)
    owned = call(functools.partial(collect_kernel, m), wide, [SMEM] + [VMEM] * 4, [VMEM] * (h + 1))(
        tile_of, *gather(*parts)
    )
    grad_x = call(
        functools.partial(inputs_kernel, m),
        jax.ShapeDtypeStruct(acts.shape, BF16),
        [VMEM] * (h + 3),
        VMEM,
        cost_estimate=pl.CostEstimate(
            flops=2 * r * acts.size, bytes_accessed=2 * acts.size, transcendentals=0
        ),
    )(owned[-1], low, *factors)
    grad_a, grad_b = call(
        functools.partial(unpack_kernel, m),
        [jax.ShapeDtypeStruct(down.shape, BF16)] * 2,
        [VMEM] * (h + 1),
        [HBM] * 2,
        scratch_shapes=[pltpu.SemaphoreType.DMA((2, m))],
    )(*exchange(*owned))
    return grad_x, grad_a, grad_b


def solution(mesh):
    placed = (
        P(("group", "fsdp"), None),
        P(("group", "fsdp"), None),
        P("fsdp", None, None),
        P("fsdp", None, None),
        P(("group", "fsdp")),
        P(),
    )
    return jax.shard_map(
        shards,
        mesh=mesh,
        in_specs=placed,
        out_specs=(
            P(("group", "fsdp"), None),
            P(("group", "fsdp"), None, None),
            P(("group", "fsdp"), None, None),
        ),
        check_vma=False,
    )
```

```python
import functools

import jax
import jax.numpy as jnp
from jax import lax
from jax.experimental import pallas as pl
from jax.experimental.pallas import tpu as pltpu
from jax.sharding import PartitionSpec as P

F32 = jnp.float32
BF16 = jnp.bfloat16
LANES = 128
ID_ROWS = 16
VMEM = pl.BlockSpec(memory_space=pltpu.VMEM)
HBM = pl.BlockSpec(memory_space=pltpu.HBM)
SMEM = pl.BlockSpec(memory_space=pltpu.SMEM)
PARAMS = pltpu.CompilerParams(vmem_limit_bytes=32 * 1024 * 1024)
ALONE = pltpu.CompilerParams(vmem_limit_bytes=60 * 1024 * 1024)


def position():
    me = lax.axis_index("fsdp")
    return me // 2, me % 2


def offsets(m):
    return [0, 1, *range(m - 1, m // 2 - 1, -1), *range(2, m // 2)]


def rank(k, m):
    return jnp.where(k < 2, k, jnp.where(k < m // 2, m // 2 + k, m + 1 - k))


def columns(chunk, w):
    return pl.ds(pl.multiple_of(chunk * w, w), w)


def pack_kernel(m, id_ref, storage_ref, down_hbm, up_hbm, *refs):
    outs, (down_ref, up_ref, out_ref, load_sems, store_sems) = refs[:m], refs[m:]
    p, _ = position()
    r, w = down_ref.shape[0], down_ref.shape[1] // m
    order = [*zip(range(m), offsets(m), outs)]
    order = order[1:] + order[:1]
    loads = []
    for i, k, _ in order:
        cols = columns(p ^ k, w)
        loads.append(
            [
                pltpu.make_async_copy(src.at[0, :, cols], dst.at[:, i * w : (i + 1) * w], sem)
                for src, dst, sem in (
                    (down_hbm, down_ref, load_sems.at[0, i]),
                    (up_hbm, up_ref, load_sems.at[1, i]),
                )
            ]
        )
        for load in loads[-1]:
            load.start()
    mark = jnp.full((ID_ROWS, LANES), storage_ref[id_ref[0]].astype(F32), F32).astype(BF16)
    stores = []
    for (i, _, dst), pair in zip(order, loads):
        for load in pair:
            load.wait()
        for b in range(w // LANES):
            cols = slice(i * w + b * LANES, i * w + (b + 1) * LANES)
            out_ref[i, 2 * r * b : 2 * r * b + r, :] = down_ref[:, cols]
            out_ref[i, 2 * r * b + r : 2 * r * (b + 1), :] = up_ref[:, cols]
        out_ref[i, 2 * r * (w // LANES) :, :] = mark
        stores.append(pltpu.make_async_copy(out_ref.at[i], dst, store_sems.at[i]))
        stores[-1].start()
    for store in stores:
        store.wait()


def stack_kernel(*refs):
    *blocks, held_ref = refs
    for at, block in enumerate(blocks):
        held_ref[at] = block[...]


def stack(blocks):
    return pl.pallas_call(
        stack_kernel,
        out_shape=jax.ShapeDtypeStruct((len(blocks), *blocks[0].shape), BF16),
        in_specs=[VMEM] * len(blocks),
        out_specs=VMEM,
        compiler_params=PARAMS,
    )(*blocks)


def pick(held, chip, here, rows):
    own_a, own_b, other_a, other_b = held
    h = own_a.shape[0]
    at = rank(chip ^ position()[0], 2 * h)
    in_a, at = at < h, lax.rem(at, h)
    own = jnp.where(in_a, own_a[at, rows, :], own_b[at, rows, :])
    other = jnp.where(in_a, other_a[at, rows, :], other_b[at, rows, :])
    return jnp.where(here, own, other)


def marks(*halves):
    h, rows, _ = halves[0].shape
    return [
        half[at, rows - ID_ROWS :, :].astype(F32)[0, 0].astype(jnp.int32)
        for half in halves
        for at in range(h)
    ]


def deliver_kernel(m, *refs):
    held, outs = refs[:4], refs[4:]
    _, c = position()
    r2 = outs[0].shape[0]
    blocks = (held[0].shape[1] - ID_ROWS) // r2
    for out, slot in zip(outs, marks(*held[:2])):
        for b in range(blocks):
            rows = slice(b * r2, (b + 1) * r2)
            out[:, b * LANES : (b + 1) * LANES] = pick(held, slot // 2, slot % 2 == c, rows)


def inverse_kernel(m, own_a, own_b, other_a, other_b, tile_of):
    p, c = position()
    for slots, core in ((marks(own_a, own_b), c), (marks(other_a, other_b), 1 - c)):
        for k, slot in zip(offsets(m), slots):
            tile_of[slot] = 2 * (p ^ k) + core


def touch_kernel(after, array, token_ref):
    token_ref[...] = jnp.zeros_like(token_ref)


def grads_kernel(m, _, acts_ref, cot_ref, *refs):
    factors, low_ref, outs = refs[:m], refs[m], refs[m + 1 :]
    p, _ = position()
    r2, w = factors[0].shape
    r = r2 // 2
    rows = acts_ref.shape[0]
    dims_nt = (((1,), (1,)), ((), ()))
    low_u = jnp.zeros((r, rows), F32)
    low_h = jnp.zeros((r, rows), F32)
    for factor, k in zip(factors, offsets(m)):
        cols = columns(p ^ k, w)
        low_u += lax.dot_general(factor[0:r, :], acts_ref[:, cols], dims_nt, preferred_element_type=F32)
        low_h += lax.dot_general(factor[r:r2, :], cot_ref[:, cols], dims_nt, preferred_element_type=F32)
    low_u = low_u.astype(BF16)
    low_h = low_h.astype(BF16)
    low_ref[...] = low_h
    for out, k in zip(outs, offsets(m)):
        cols = columns(p ^ k, w)
        out[0:r, :] = jnp.dot(low_h, acts_ref[:, cols], preferred_element_type=F32).astype(BF16)
        out[r:r2, :] = jnp.dot(low_u, cot_ref[:, cols], preferred_element_type=F32).astype(BF16)


def inputs_kernel(m, _, low_ref, *refs):
    factors, gx_ref = refs[:m], refs[m]
    p, _ = position()
    r2, w = factors[0].shape
    for factor, k in zip(factors, offsets(m)):
        gx_ref[:, columns(p ^ k, w)] = lax.dot_general(
            low_ref[...], factor[0 : r2 // 2, :], (((0,), (0,)), ((), ())), preferred_element_type=F32
        ).astype(BF16)


def collect_kernel(m, tile_of, *refs):
    held, outs = refs[:4], refs[4:]
    p, c = position()
    for out, k in zip(outs, offsets(m)):
        tile = tile_of[2 * (p ^ k) + c]
        out[...] = pick(held, tile // 2, tile % 2 == c, slice(None))


def unpack_kernel(m, *refs):
    ga_ref, gb_ref = refs[m:]
    p, _ = position()
    r2, w = refs[0].shape
    for block, k in zip(refs, offsets(m)):
        cols = columns(p ^ k, w)
        ga_ref[0, :, cols] = block[0 : r2 // 2, :]
        gb_ref[0, :, cols] = block[r2 // 2 : r2, :]


def shards(acts, cotangent, down, up, adapter_per_tile, adapter_storage_slot):
    n = lax.axis_size("fsdp")
    m = n // 2
    _, r, d = down.shape
    w = d // m

    def exchange(blocks):
        return [blocks[0]] + [
            lax.ppermute(
                block, "fsdp", [(2 * p + c, 2 * (p ^ k) + c) for p in range(m) for c in range(2)]
            )
            for block, k in zip(blocks[1:], offsets(m)[1:])
        ]

    def gather(blocks):
        own = [stack(blocks[: m // 2]), stack(blocks[m // 2 :])]
        return own + [lax.ppermute(half, "fsdp", [(f, f ^ 1) for f in range(n)]) for half in own]

    rows = 2 * r * w // LANES
    flat = jax.ShapeDtypeStruct((rows + ID_ROWS, LANES), BF16)
    wide = jax.ShapeDtypeStruct((2 * r, w), BF16)
    spread = pl.pallas_call(
        functools.partial(pack_kernel, m),
        out_shape=[flat] * m,
        in_specs=[SMEM, SMEM, HBM, HBM],
        out_specs=[HBM] * m,
        scratch_shapes=[
            pltpu.VMEM((r, d), BF16),
            pltpu.VMEM((r, d), BF16),
            pltpu.VMEM((m, *flat.shape), BF16),
            pltpu.SemaphoreType.DMA((2, m)),
            pltpu.SemaphoreType.DMA((m,)),
        ],
        compiler_params=ALONE,
    )(adapter_per_tile, adapter_storage_slot, down, up)
    held = gather(exchange(spread))
    factors = pl.pallas_call(
        functools.partial(deliver_kernel, m),
        out_shape=[wide] * m,
        in_specs=[VMEM] * 4,
        out_specs=[VMEM] * m,
        compiler_params=PARAMS,
    )(*held)
    token = pl.pallas_call(
        touch_kernel,
        out_shape=jax.ShapeDtypeStruct((8, LANES), F32),
        in_specs=[VMEM, VMEM],
        out_specs=VMEM,
        compiler_params=PARAMS,
    )(factors[-1], cotangent)
    factors = exchange(factors)
    tile_of = pl.pallas_call(
        functools.partial(inverse_kernel, m),
        out_shape=jax.ShapeDtypeStruct((n,), jnp.int32),
        in_specs=[VMEM] * 4,
        out_specs=SMEM,
        compiler_params=PARAMS,
    )(*held)
    low, *parts = pl.pallas_call(
        functools.partial(grads_kernel, m),
        out_shape=[jax.ShapeDtypeStruct((r, acts.shape[0]), BF16)] + [wide] * m,
        in_specs=[VMEM] * (m + 3),
        out_specs=[VMEM] * (m + 1),
        compiler_params=PARAMS,
    )(token, acts, cotangent, *factors)
    parts = exchange(parts)
    owned = pl.pallas_call(
        functools.partial(collect_kernel, m),
        out_shape=[wide] * m,
        in_specs=[SMEM] + [VMEM] * 4,
        out_specs=[VMEM] * m,
        compiler_params=PARAMS,
    )(tile_of, *gather(parts))
    grad_x = pl.pallas_call(
        functools.partial(inputs_kernel, m),
        out_shape=jax.ShapeDtypeStruct(acts.shape, BF16),
        in_specs=[VMEM] * (m + 2),
        out_specs=VMEM,
        compiler_params=PARAMS,
        cost_estimate=pl.CostEstimate(
            flops=2 * r * acts.size, bytes_accessed=2 * acts.size, transcendentals=0
        ),
    )(owned[-1], low, *factors)
    grad_a, grad_b = pl.pallas_call(
        functools.partial(unpack_kernel, m),
        out_shape=[jax.ShapeDtypeStruct(down.shape, BF16)] * 2,
        in_specs=[VMEM] * m,
        out_specs=[VMEM] * 2,
        compiler_params=PARAMS,
    )(*exchange(owned))
    return grad_x, grad_a, grad_b


def solution(mesh):
    placed = (
        P(("group", "fsdp"), None),
        P(("group", "fsdp"), None),
        P("fsdp", None, None),
        P("fsdp", None, None),
        P(("group", "fsdp")),
        P(),
    )
    return jax.shard_map(
        shards,
        mesh=mesh,
        in_specs=placed,
        out_specs=(
            P(("group", "fsdp"), None),
            P(("group", "fsdp"), None, None),
            P(("group", "fsdp"), None, None),
        ),
        check_vma=False,
    )
```

```python
import functools

import jax
import jax.numpy as jnp
from jax import lax
from jax.experimental import pallas as pl
from jax.experimental.pallas import tpu as pltpu
from jax.sharding import PartitionSpec as P

F32 = jnp.float32
BF16 = jnp.bfloat16
LANES = 128
ID_ROWS = 16
VMEM = pl.BlockSpec(memory_space=pltpu.VMEM)
HBM = pl.BlockSpec(memory_space=pltpu.HBM)
SMEM = pl.BlockSpec(memory_space=pltpu.SMEM)
PARAMS = pltpu.CompilerParams(vmem_limit_bytes=32 * 1024 * 1024)
ALONE = pltpu.CompilerParams(vmem_limit_bytes=60 * 1024 * 1024)


def position():
    me = lax.axis_index("fsdp")
    return me // 2, me % 2


def offsets(m):
    return [0, 1, *range(m - 1, m // 2 - 1, -1), *range(2, m // 2)]


def rank(k, m):
    return jnp.where(k < 2, k, jnp.where(k < m // 2, m // 2 + k, m + 1 - k))


def deliveries(groups, h):
    pairs = [(x, k) for x in range(groups) for k in range(h)]
    return sorted(pairs, key=lambda pair: (pair[0].bit_count() + pair[1].bit_count(), pair))


def share(groups, h, x, k):
    return (lax.axis_index("group") ^ x) * h + (lax.rem(position()[0], h) ^ k)


def columns(chunk, w):
    return pl.ds(pl.multiple_of(chunk * w, w), w)


def pack_kernel(groups, h, id_ref, storage_ref, down_hbm, up_hbm, *refs):
    outs, (down_ref, up_ref, out_ref, load_sems, store_sems) = refs[:h], refs[h:]
    r, w = down_ref.shape[0], down_ref.shape[1] // h
    loads = []
    for k in range(h):
        cols = columns(share(groups, h, 0, k), w)
        loads.append(
            [
                pltpu.make_async_copy(src.at[0, :, cols], dst.at[:, k * w : (k + 1) * w], sem)
                for src, dst, sem in (
                    (down_hbm, down_ref, load_sems.at[0, k]),
                    (up_hbm, up_ref, load_sems.at[1, k]),
                )
            ]
        )
        for load in loads[-1]:
            load.start()
    mark = jnp.full((ID_ROWS, LANES), storage_ref[id_ref[0]].astype(F32), F32).astype(BF16)
    stores = []
    for k, (dst, pair) in enumerate(zip(outs, loads)):
        for load in pair:
            load.wait()
        for b in range(w // LANES):
            cols = slice(k * w + b * LANES, k * w + (b + 1) * LANES)
            out_ref[k, 2 * r * b : 2 * r * b + r, :] = down_ref[:, cols]
            out_ref[k, 2 * r * b + r : 2 * r * (b + 1), :] = up_ref[:, cols]
        out_ref[k, 2 * r * (w // LANES) :, :] = mark
        stores.append(pltpu.make_async_copy(out_ref.at[k], dst, store_sems.at[k]))
        stores[-1].start()
    for store in stores:
        store.wait()


def stack_kernel(h, *refs):
    held_ref = refs[-1]
    for at, block in enumerate(refs[:h]):
        held_ref[at] = block[...]


def near_kernel(*refs):
    *blocks, held_ref, marks_ref = refs
    for at, block in enumerate(blocks):
        held_ref[at] = block[...]
        marks_ref[at] = block[block.shape[0] - ID_ROWS :, :]


def pick(held, at, here, rows):
    own_a, own_b, other_a, other_b = held
    h = own_a.shape[0]
    in_a, at = at < h, lax.rem(at, h)
    own = jnp.where(in_a, own_a[at, rows, :], own_b[at, rows, :])
    other = jnp.where(in_a, other_a[at, rows, :], other_b[at, rows, :])
    return jnp.where(here, own, other)


def slots_of(held_ref):
    h, rows, _ = held_ref.shape
    return [
        held_ref[at, rows - ID_ROWS :, :].astype(F32)[0, 0].astype(jnp.int32) for at in range(h)
    ]


def deliver_kernel(groups, *refs):
    held, marks, outs = refs[:4], refs[4 : groups + 3], refs[groups + 3 :]
    p, c = position()
    h = held[0].shape[0]
    r2, w = outs[0].shape
    slots = [slots_of(held[0])] + [slots_of(mark) for mark in marks]
    for out, (x, k) in zip(outs, deliveries(groups, h)):
        slot = slots[x][k]
        for b in range(w // LANES):
            rows = slice(b * r2, (b + 1) * r2)
            out[:, b * LANES : (b + 1) * LANES] = pick(held, (slot // 2) ^ p, slot % 2 == c, rows)


def inverse_kernel(own_a, own_b, other_a, other_b, tile_of):
    p, c = position()
    for near, far, core in ((own_a, own_b, c), (other_a, other_b, 1 - c)):
        for k, slot in enumerate(slots_of(near) + slots_of(far)):
            tile_of[slot] = 2 * (p ^ k) + core


def touch_kernel(after, array, token_ref):
    token_ref[...] = jnp.zeros_like(token_ref)


def grads_kernel(m, groups, _, acts_ref, cot_ref, *refs):
    ways = deliveries(groups, m // 2)
    factors, low_ref, outs = refs[: len(ways)], refs[len(ways)], refs[len(ways) + 1 :]
    p, _ = position()
    r2, w = factors[0].shape
    r = r2 // 2
    rows = acts_ref.shape[0]
    dims_nt = (((1,), (1,)), ((), ()))
    low_u = jnp.zeros((r, rows), F32)
    low_h = jnp.zeros((r, rows), F32)
    for (x, k), factor in zip(ways, factors):
        cols = columns(share(groups, m // 2, x, k), w)
        low_u += lax.dot_general(factor[0:r, :], acts_ref[:, cols], dims_nt, preferred_element_type=F32)
        low_h += lax.dot_general(factor[r:r2, :], cot_ref[:, cols], dims_nt, preferred_element_type=F32)
    low_u = low_u.astype(BF16)
    low_h = low_h.astype(BF16)
    low_ref[...] = low_h
    for k, out in zip(offsets(m), outs):
        cols = columns(p ^ k, out.shape[1])
        out[0:r, :] = jnp.dot(low_h, acts_ref[:, cols], preferred_element_type=F32).astype(BF16)
        out[r:r2, :] = jnp.dot(low_u, cot_ref[:, cols], preferred_element_type=F32).astype(BF16)


def inputs_kernel(m, groups, _, low_ref, *refs):
    *factors, gx_ref = refs
    for (x, k), factor in zip(deliveries(groups, m // 2), factors):
        r2, w = factor.shape
        gx_ref[:, columns(share(groups, m // 2, x, k), w)] = lax.dot_general(
            low_ref[...], factor[0 : r2 // 2, :], (((0,), (0,)), ((), ())), preferred_element_type=F32
        ).astype(BF16)


def collect_kernel(m, tile_of, *refs):
    held, outs = refs[:4], refs[4:]
    p, c = position()
    for out, k in zip(outs, offsets(m)):
        tile = tile_of[2 * (p ^ k) + c]
        out[...] = pick(held, rank((tile // 2) ^ p, m), tile % 2 == c, slice(None))


def unpack_kernel(m, *refs):
    ga_ref, gb_ref = refs[m:]
    p, _ = position()
    r2, w = refs[0].shape
    for block, k in zip(refs, offsets(m)):
        cols = columns(p ^ k, w)
        ga_ref[0, :, cols] = block[0 : r2 // 2, :]
        gb_ref[0, :, cols] = block[r2 // 2 : r2, :]


def call(kernel, out_shape, in_specs, out_specs, params=PARAMS, **options):
    return pl.pallas_call(
        kernel,
        out_shape=out_shape,
        in_specs=in_specs,
        out_specs=out_specs,
        compiler_params=params,
        **options,
    )


def bf16(*shape):
    return jax.ShapeDtypeStruct(shape, BF16)


def shards(acts, cotangent, down, up, adapter_per_tile, adapter_storage_slot):
    groups, n = lax.axis_size("group"), lax.axis_size("fsdp")
    m, h = n // 2, n // 4
    _, r, d = down.shape

    def to_chip(k, block):
        pairs = [(2 * p + c, 2 * (p ^ k) + c) for p in range(m) for c in range(2)]
        return lax.ppermute(block, "fsdp", pairs)

    def to_device(x, k, block):
        pairs = [
            (g * n + 2 * p + c, (g ^ x) * n + 2 * (p ^ k) + c)
            for g in range(groups)
            for p in range(m)
            for c in range(2)
        ]
        return lax.ppermute(block, ("group", "fsdp"), pairs)

    def exchange(blocks):
        return [blocks[0]] + [to_chip(k, block) for block, k in zip(blocks[1:], offsets(m)[1:])]

    def with_other_core(*own):
        return [*own, *(lax.ppermute(half, "fsdp", [(f, f ^ 1) for f in range(n)]) for half in own)]

    def stack(blocks, *after):
        count = len(blocks) + len(after)
        return call(
            functools.partial(stack_kernel, h), bf16(h, *blocks[0].shape), [VMEM] * count, VMEM
        )(*blocks, *after)

    ways = deliveries(groups, h)
    w = d // len(ways)
    flat = bf16(2 * r * w // LANES + ID_ROWS, LANES)
    spread = call(
        functools.partial(pack_kernel, groups, h),
        [flat] * h,
        [SMEM, SMEM, HBM, HBM],
        [HBM] * h,
        ALONE,
        scratch_shapes=[
            pltpu.VMEM((r, h * w), BF16),
            pltpu.VMEM((r, h * w), BF16),
            pltpu.VMEM((h, *flat.shape), BF16),
            pltpu.SemaphoreType.DMA((2, h)),
            pltpu.SemaphoreType.DMA((h,)),
        ],
    )(adapter_per_tile, adapter_storage_slot, down, up)
    near = [spread[0]] + [to_chip(k, spread[k]) for k in range(1, h)]
    far = [to_chip(h, block) for block in near]
    near, marks = call(
        near_kernel, [bf16(h, *flat.shape), bf16(h, ID_ROWS, LANES)], [VMEM] * h, [VMEM] * 2
    )(*near)
    marks = [to_device(x, 0, marks) for x in range(1, groups)]
    held = with_other_core(near, stack(far, *marks))
    factors = call(
        functools.partial(deliver_kernel, groups),
        [bf16(2 * r, w)] * len(ways),
        [VMEM] * (groups + 3),
        [VMEM] * len(ways),
    )(*held, *marks)
    token = call(touch_kernel, jax.ShapeDtypeStruct((8, LANES), F32), [VMEM] * 2, VMEM)(
        factors[-1], cotangent
    )
    factors = [factors[0]] + [
        to_device(x, k, block) for (x, k), block in zip(ways[1:], factors[1:])
    ]
    tile_of = call(inverse_kernel, jax.ShapeDtypeStruct((n,), jnp.int32), [VMEM] * 4, SMEM)(*held)

    wide = bf16(2 * r, d // m)
    low, *parts = call(
        functools.partial(grads_kernel, m, groups),
        [bf16(r, acts.shape[0])] + [wide] * m,
        [VMEM] * (len(ways) + 3),
        [VMEM] * (m + 1),
    )(token, acts, cotangent, *factors)
    parts = exchange(parts)
    owned = call(functools.partial(collect_kernel, m), [wide] * m, [SMEM] + [VMEM] * 4, [VMEM] * m)(
        tile_of, *with_other_core(stack(parts[:h]), stack(parts[h:]))
    )
    grad_x = call(
        functools.partial(inputs_kernel, m, groups),
        bf16(*acts.shape),
        [VMEM] * (len(ways) + 2),
        VMEM,
        cost_estimate=pl.CostEstimate(
            flops=2 * r * acts.size, bytes_accessed=2 * acts.size, transcendentals=0
        ),
    )(owned[-1], low, *factors)
    grad_a, grad_b = call(
        functools.partial(unpack_kernel, m), [bf16(*down.shape)] * 2, [VMEM] * m, [VMEM] * 2
    )(*exchange(owned))
    return grad_x, grad_a, grad_b


def solution(mesh):
    placed = (
        P(("group", "fsdp"), None),
        P(("group", "fsdp"), None),
        P("fsdp", None, None),
        P("fsdp", None, None),
        P(("group", "fsdp")),
        P(),
    )
    return jax.shard_map(
        shards,
        mesh=mesh,
        in_specs=placed,
        out_specs=(
            P(("group", "fsdp"), None),
            P(("group", "fsdp"), None, None),
            P(("group", "fsdp"), None, None),
        ),
        check_vma=False,
    )
```

```python
import functools

import jax
import jax.numpy as jnp
from jax import lax
from jax.experimental import pallas as pl
from jax.experimental.pallas import tpu as pltpu
from jax.sharding import PartitionSpec as P

F32 = jnp.float32
BF16 = jnp.bfloat16
LANES = 128
ID_ROWS = 16
VMEM = pl.BlockSpec(memory_space=pltpu.VMEM)
HBM = pl.BlockSpec(memory_space=pltpu.HBM)
SMEM = pl.BlockSpec(memory_space=pltpu.SMEM)
PARAMS = pltpu.CompilerParams(vmem_limit_bytes=32 * 1024 * 1024)
ALONE = pltpu.CompilerParams(vmem_limit_bytes=60 * 1024 * 1024)


def position():
    me = lax.axis_index("fsdp")
    return me // 2, me % 2


def offsets(m):
    return [0, 1, *range(m - 1, m // 2 - 1, -1), *range(2, m // 2)]


def rank(k, m):
    return jnp.where(k < 2, k, jnp.where(k < m // 2, m // 2 + k, m + 1 - k))


def deliveries(groups, h):
    pairs = [(x, k) for x in range(groups) for k in range(h)]
    far = sorted(pairs[1:], key=lambda pair: (-pair[0].bit_count() - pair[1].bit_count(), pair))
    return pairs[:1] + far


def share(groups, h, x, k):
    return (lax.axis_index("group") ^ x) * h + (lax.rem(position()[0], h) ^ k)


def columns(chunk, w):
    return pl.ds(pl.multiple_of(chunk * w, w), w)


def pack_kernel(groups, h, id_ref, storage_ref, down_hbm, up_hbm, *refs):
    outs, (down_ref, up_ref, out_ref, load_sems, store_sems) = refs[:h], refs[h:]
    r, w = down_ref.shape[0], down_ref.shape[1] // h
    first = outs[0].shape[0]
    loads = []
    for k in range(h):
        cols = columns(share(groups, h, 0, k), w)
        loads.append(
            [
                pltpu.make_async_copy(src.at[0, :, cols], dst.at[:, k * w : (k + 1) * w], sem)
                for src, dst, sem in (
                    (down_hbm, down_ref, load_sems.at[0, k]),
                    (up_hbm, up_ref, load_sems.at[1, k]),
                )
            ]
        )
        for load in loads[-1]:
            load.start()
    mark = jnp.full((ID_ROWS, LANES), storage_ref[id_ref[0]].astype(F32), F32).astype(BF16)
    stores = []
    for k, pair in enumerate(loads):
        for load in pair:
            load.wait()
        for b in range(w // LANES):
            cols = slice(k * w + b * LANES, k * w + (b + 1) * LANES)
            out_ref[k, 2 * r * b : 2 * r * b + r, :] = down_ref[:, cols]
            out_ref[k, 2 * r * b + r : 2 * r * (b + 1), :] = up_ref[:, cols]
        out_ref[k, 2 * r * (w // LANES) :, :] = mark
        dsts = [outs[0].at[k]] * (k < first) + [outs[k]] * (k > 0)
        for i, dst in enumerate(dsts):
            stores.append(pltpu.make_async_copy(out_ref.at[k], dst, store_sems.at[i, k]))
            stores[-1].start()
    for store in stores:
        store.wait()


def block_of(ref):
    return ref[0] if len(ref.shape) == 3 else ref[...]


def stack_kernel(h, *refs):
    held_ref = refs[-1]
    for at, ref in enumerate(refs[:h]):
        held_ref[at] = block_of(ref)


def split_kernel(array_ref, *outs):
    for at, out in enumerate(outs):
        out[...] = array_ref[at + 1]


def near_kernel(*refs):
    *blocks, held_ref, marks_ref = refs
    for at, ref in enumerate(blocks):
        block = block_of(ref)
        held_ref[at] = block
        marks_ref[at] = block[block.shape[0] - ID_ROWS :, :]


def pick(held, at, here, rows):
    own_a, own_b, other_a, other_b = held
    h = own_a.shape[0]
    in_a, at = at < h, lax.rem(at, h)
    own = jnp.where(in_a, own_a[at, rows, :], own_b[at, rows, :])
    other = jnp.where(in_a, other_a[at, rows, :], other_b[at, rows, :])
    return jnp.where(here, own, other)


def slots_of(held_ref):
    h, rows, _ = held_ref.shape
    return [
        held_ref[at, rows - ID_ROWS :, :].astype(F32)[0, 0].astype(jnp.int32) for at in range(h)
    ]


def deliver_kernel(groups, *refs):
    held, marks, outs = refs[:4], refs[4 : groups + 3], refs[groups + 3 :]
    p, c = position()
    h = held[0].shape[0]
    r2, w = outs[0].shape
    slots = [slots_of(held[0])] + [slots_of(mark) for mark in marks]
    for out, (x, k) in zip(outs, deliveries(groups, h)):
        slot = slots[x][k]
        for b in range(w // LANES):
            rows = slice(b * r2, (b + 1) * r2)
            out[:, b * LANES : (b + 1) * LANES] = pick(held, (slot // 2) ^ p, slot % 2 == c, rows)


def inverse_kernel(own_a, own_b, other_a, other_b, tile_of):
    p, c = position()
    for near, far, core in ((own_a, own_b, c), (other_a, other_b, 1 - c)):
        for k, slot in enumerate(slots_of(near) + slots_of(far)):
            tile_of[slot] = 2 * (p ^ k) + core


def touch_kernel(after, array, token_ref):
    token_ref[...] = jnp.zeros_like(token_ref)


def grads_kernel(m, groups, _, acts_ref, cot_ref, *refs):
    ways = deliveries(groups, m // 2)
    factors, low_ref, outs = refs[: len(ways)], refs[len(ways)], refs[len(ways) + 1 :]
    p, _ = position()
    r2, w = factors[0].shape
    r = r2 // 2
    rows = acts_ref.shape[0]
    dims_nt = (((1,), (1,)), ((), ()))
    low_u = jnp.zeros((r, rows), F32)
    low_h = jnp.zeros((r, rows), F32)
    for (x, k), factor in zip(ways, factors):
        cols = columns(share(groups, m // 2, x, k), w)
        low_u += lax.dot_general(factor[0:r, :], acts_ref[:, cols], dims_nt, preferred_element_type=F32)
        low_h += lax.dot_general(factor[r:r2, :], cot_ref[:, cols], dims_nt, preferred_element_type=F32)
    low_u = low_u.astype(BF16)
    low_h = low_h.astype(BF16)
    low_ref[...] = low_h
    for k, out in zip(offsets(m), outs):
        cols = columns(p ^ k, out.shape[1])
        out[0:r, :] = jnp.dot(low_h, acts_ref[:, cols], preferred_element_type=F32).astype(BF16)
        out[r:r2, :] = jnp.dot(low_u, cot_ref[:, cols], preferred_element_type=F32).astype(BF16)


def inputs_kernel(m, groups, _, low_ref, *refs):
    *factors, gx_ref = refs
    for (x, k), factor in zip(deliveries(groups, m // 2), factors):
        r2, w = factor.shape
        gx_ref[:, columns(share(groups, m // 2, x, k), w)] = lax.dot_general(
            low_ref[...], factor[0 : r2 // 2, :], (((0,), (0,)), ((), ())), preferred_element_type=F32
        ).astype(BF16)


def collect_kernel(m, tile_of, *refs):
    held, outs = refs[:4], refs[4:]
    p, c = position()
    for out, k in zip(outs, offsets(m)):
        tile = tile_of[2 * (p ^ k) + c]
        out[...] = pick(held, rank((tile // 2) ^ p, m), tile % 2 == c, slice(None))


def unpack_kernel(m, *refs):
    ga_ref, gb_ref = refs[m:]
    p, _ = position()
    r2, w = refs[0].shape
    for block, k in zip(refs, offsets(m)):
        cols = columns(p ^ k, w)
        ga_ref[0, :, cols] = block[0 : r2 // 2, :]
        gb_ref[0, :, cols] = block[r2 // 2 : r2, :]


def call(kernel, out_shape, in_specs, out_specs, params=PARAMS, **options):
    return pl.pallas_call(
        kernel,
        out_shape=out_shape,
        in_specs=in_specs,
        out_specs=out_specs,
        compiler_params=params,
        **options,
    )


def bf16(*shape):
    return jax.ShapeDtypeStruct(shape, BF16)


def shards(acts, cotangent, down, up, adapter_per_tile, adapter_storage_slot):
    groups, n = lax.axis_size("group"), lax.axis_size("fsdp")
    m, h = n // 2, n // 4
    _, r, d = down.shape

    def to_chip(k, block):
        pairs = [(2 * p + c, 2 * (p ^ k) + c) for p in range(m) for c in range(2)]
        return lax.ppermute(block, "fsdp", pairs)

    def to_device(x, k, block):
        pairs = [
            (g * n + 2 * p + c, (g ^ x) * n + 2 * (p ^ k) + c)
            for g in range(groups)
            for p in range(m)
            for c in range(2)
        ]
        return lax.ppermute(block, ("group", "fsdp"), pairs)

    def exchange(blocks):
        return [blocks[0]] + [to_chip(k, block) for block, k in zip(blocks[1:], offsets(m)[1:])]

    def with_other_core(*own):
        return [*own, *(lax.ppermute(half, "fsdp", [(f, f ^ 1) for f in range(n)]) for half in own)]

    def stack(blocks, *after):
        count = len(blocks) + len(after)
        return call(
            functools.partial(stack_kernel, h), bf16(h, *blocks[-1].shape), [VMEM] * count, VMEM
        )(*blocks, *after)

    ways = deliveries(groups, h)
    w = d // len(ways)
    flat = bf16(2 * r * w // LANES + ID_ROWS, LANES)
    spread = call(
        functools.partial(pack_kernel, groups, h),
        [bf16(h // 2, *flat.shape)] + [flat] * (h - 1),
        [SMEM, SMEM, HBM, HBM],
        [HBM] * h,
        ALONE,
        scratch_shapes=[
            pltpu.VMEM((r, h * w), BF16),
            pltpu.VMEM((r, h * w), BF16),
            pltpu.VMEM((h, *flat.shape), BF16),
            pltpu.SemaphoreType.DMA((2, h)),
            pltpu.SemaphoreType.DMA((2, h)),
        ],
    )(adapter_per_tile, adapter_storage_slot, down, up)
    crossed = to_chip(h, spread[0])
    near = [spread[0]] + [to_chip(k, spread[k]) for k in range(1, h)]
    handed = call(split_kernel, [flat] * (h // 2 - 1), [VMEM], [VMEM] * (h // 2 - 1))(crossed)
    far = [crossed] + [to_chip(k + 1, block) for k, block in enumerate(handed)]
    far += [to_chip(h, block) for block in near[h // 2 :]]
    near, marks = call(
        near_kernel, [bf16(h, *flat.shape), bf16(h, ID_ROWS, LANES)], [VMEM] * h, [VMEM] * 2
    )(*near)
    marks = [to_device(x, 0, marks) for x in range(1, groups)]
    held = with_other_core(near, stack(far, *marks))
    factors = call(
        functools.partial(deliver_kernel, groups),
        [bf16(2 * r, w)] * len(ways),
        [VMEM] * (groups + 3),
        [VMEM] * len(ways),
    )(*held, *marks)
    token = call(touch_kernel, jax.ShapeDtypeStruct((8, LANES), F32), [VMEM] * 2, VMEM)(
        factors[-1], cotangent
    )
    factors = [factors[0]] + [
        to_device(x, k, block) for (x, k), block in zip(ways[1:], factors[1:])
    ]
    tile_of = call(inverse_kernel, jax.ShapeDtypeStruct((n,), jnp.int32), [VMEM] * 4, SMEM)(*held)

    wide = bf16(2 * r, d // m)
    low, *parts = call(
        functools.partial(grads_kernel, m, groups),
        [bf16(r, acts.shape[0])] + [wide] * m,
        [VMEM] * (len(ways) + 3),
        [VMEM] * (m + 1),
    )(token, acts, cotangent, *factors)
    parts = exchange(parts)
    owned = call(functools.partial(collect_kernel, m), [wide] * m, [SMEM] + [VMEM] * 4, [VMEM] * m)(
        tile_of, *with_other_core(stack(parts[:h]), stack(parts[h:]))
    )
    grad_x = call(
        functools.partial(inputs_kernel, m, groups),
        bf16(*acts.shape),
        [VMEM] * (len(ways) + 2),
        VMEM,
        cost_estimate=pl.CostEstimate(
            flops=2 * r * acts.size, bytes_accessed=2 * acts.size, transcendentals=0
        ),
    )(owned[-1], low, *factors)
    grad_a, grad_b = call(
        functools.partial(unpack_kernel, m), [bf16(*down.shape)] * 2, [VMEM] * m, [VMEM] * 2
    )(*exchange(owned))
    return grad_x, grad_a, grad_b


def solution(mesh):
    placed = (
        P(("group", "fsdp"), None),
        P(("group", "fsdp"), None),
        P("fsdp", None, None),
        P("fsdp", None, None),
        P(("group", "fsdp")),
        P(),
    )
    return jax.shard_map(
        shards,
        mesh=mesh,
        in_specs=placed,
        out_specs=(
            P(("group", "fsdp"), None),
            P(("group", "fsdp"), None, None),
            P(("group", "fsdp"), None, None),
        ),
        check_vma=False,
    )
```

```python
import functools

import jax
import jax.numpy as jnp
from jax import lax
from jax.experimental import pallas as pl
from jax.experimental.pallas import tpu as pltpu
from jax.sharding import PartitionSpec as P

F32 = jnp.float32
BF16 = jnp.bfloat16
LANES = 128
ID_ROWS = 16
VMEM = pl.BlockSpec(memory_space=pltpu.VMEM)
HBM = pl.BlockSpec(memory_space=pltpu.HBM)
SMEM = pl.BlockSpec(memory_space=pltpu.SMEM)
PARAMS = pltpu.CompilerParams(vmem_limit_bytes=32 * 1024 * 1024)
ALONE = pltpu.CompilerParams(vmem_limit_bytes=60 * 1024 * 1024)


def position():
    me = lax.axis_index("fsdp")
    return me // 2, me % 2


def offsets(m):
    near, far = [*range(1, m // 2)], [*range(m - 1, m // 2 - 1, -1)]
    return [0, far[0], near[0], far[1], near[1], *far[2:], *near[2:]]


def rank(k, m):
    near = jnp.where(k < 3, 2 * k, m // 2 + k)
    far = jnp.where(k > m - 3, 2 * (m - 1 - k) + 1, m + 2 - k)
    return jnp.where(k < m // 2, near, far)


def deliveries(groups, h):
    pairs = [(x, k) for x in range(groups) for k in range(h)]
    far = sorted(pairs[1:], key=lambda pair: (-pair[0].bit_count() - pair[1].bit_count(), pair))
    return pairs[:1] + far


def share(groups, h, x, k):
    return (lax.axis_index("group") ^ x) * h + (lax.rem(position()[0], h) ^ k)


def columns(chunk, w):
    return pl.ds(pl.multiple_of(chunk * w, w), w)


def pack_kernel(groups, h, id_ref, storage_ref, down_hbm, up_hbm, *refs):
    outs, (down_ref, up_ref, out_ref, load_sems, store_sems) = refs[: h + 1], refs[h + 1 :]
    r, w = down_ref.shape[0], down_ref.shape[1] // h
    first = outs[0].shape[0]
    loads = []
    for k in range(h):
        cols = columns(share(groups, h, 0, k), w)
        loads.append(
            [
                pltpu.make_async_copy(src.at[0, :, cols], dst.at[:, k * w : (k + 1) * w], sem)
                for src, dst, sem in (
                    (down_hbm, down_ref, load_sems.at[0, k]),
                    (up_hbm, up_ref, load_sems.at[1, k]),
                )
            ]
        )
        for load in loads[-1]:
            load.start()
    mark = jnp.full((ID_ROWS, LANES), storage_ref[id_ref[0]].astype(F32), F32).astype(BF16)
    stores = []
    for k, pair in enumerate(loads):
        for load in pair:
            load.wait()
        for b in range(w // LANES):
            cols = slice(k * w + b * LANES, k * w + (b + 1) * LANES)
            out_ref[k, 2 * r * b : 2 * r * b + r, :] = down_ref[:, cols]
            out_ref[k, 2 * r * b + r : 2 * r * (b + 1), :] = up_ref[:, cols]
        out_ref[k, 2 * r * (w // LANES) :, :] = mark
        dsts = [outs[k + 1]] + ([outs[0].at[k - 1]] if 0 < k <= first else [])
        for i, dst in enumerate(dsts):
            stores.append(pltpu.make_async_copy(out_ref.at[k], dst, store_sems.at[i, k]))
            stores[-1].start()
    for store in stores:
        store.wait()


def stack_kernel(h, *refs):
    held_ref = refs[-1]
    for at, ref in enumerate(refs[:h]):
        held_ref[at] = ref[...]


def split_kernel(array_ref, *outs):
    for at, out in enumerate(outs):
        out[...] = array_ref[at]


def near_kernel(*refs):
    *blocks, held_ref, marks_ref = refs
    for at, ref in enumerate(blocks):
        block = ref[...]
        held_ref[at] = block
        marks_ref[at] = block[block.shape[0] - ID_ROWS :, :]


def pick(held, at, here, rows):
    own_a, own_b, other_a, other_b = held
    h = own_a.shape[0]
    in_a, at = at < h, lax.rem(at, h)
    own = jnp.where(in_a, own_a[at, rows, :], own_b[at, rows, :])
    other = jnp.where(in_a, other_a[at, rows, :], other_b[at, rows, :])
    return jnp.where(here, own, other)


def slots_of(held_ref):
    h, rows, _ = held_ref.shape
    return [
        held_ref[at, rows - ID_ROWS :, :].astype(F32)[0, 0].astype(jnp.int32) for at in range(h)
    ]


def deliver_kernel(groups, *refs):
    held, marks, outs = refs[:4], refs[4 : groups + 3], refs[groups + 3 :]
    p, c = position()
    h = held[0].shape[0]
    r2, w = outs[0].shape
    slots = [slots_of(held[0])] + [slots_of(mark) for mark in marks]
    for out, (x, k) in zip(outs, deliveries(groups, h)):
        slot = slots[x][k]
        for b in range(w // LANES):
            rows = slice(b * r2, (b + 1) * r2)
            out[:, b * LANES : (b + 1) * LANES] = pick(held, (slot // 2) ^ p, slot % 2 == c, rows)


def inverse_kernel(own_a, own_b, other_a, other_b, tile_of):
    p, c = position()
    for near, far, core in ((own_a, own_b, c), (other_a, other_b, 1 - c)):
        for k, slot in enumerate(slots_of(near) + slots_of(far)):
            tile_of[slot] = 2 * (p ^ k) + core


def touch_kernel(after, array, token_ref):
    token_ref[...] = jnp.zeros_like(token_ref)


def grads_kernel(m, groups, _, acts_ref, cot_ref, *refs):
    ways = deliveries(groups, m // 2)
    factors, low_ref, outs = refs[: len(ways)], refs[len(ways)], refs[len(ways) + 1 :]
    p, _ = position()
    r2, w = factors[0].shape
    r = r2 // 2
    rows = acts_ref.shape[0]
    dims_nt = (((1,), (1,)), ((), ()))
    low_u = jnp.zeros((r, rows), F32)
    low_h = jnp.zeros((r, rows), F32)
    for (x, k), factor in zip(ways, factors):
        cols = columns(share(groups, m // 2, x, k), w)
        low_u += lax.dot_general(factor[0:r, :], acts_ref[:, cols], dims_nt, preferred_element_type=F32)
        low_h += lax.dot_general(factor[r:r2, :], cot_ref[:, cols], dims_nt, preferred_element_type=F32)
    low_u = low_u.astype(BF16)
    low_h = low_h.astype(BF16)
    low_ref[...] = low_h
    for k, out in zip(offsets(m), outs):
        cols = columns(p ^ k, out.shape[1])
        out[0:r, :] = jnp.dot(low_h, acts_ref[:, cols], preferred_element_type=F32).astype(BF16)
        out[r:r2, :] = jnp.dot(low_u, cot_ref[:, cols], preferred_element_type=F32).astype(BF16)


def inputs_kernel(m, groups, _, low_ref, *refs):
    *factors, gx_ref = refs
    for (x, k), factor in zip(deliveries(groups, m // 2), factors):
        r2, w = factor.shape
        gx_ref[:, columns(share(groups, m // 2, x, k), w)] = lax.dot_general(
            low_ref[...], factor[0 : r2 // 2, :], (((0,), (0,)), ((), ())), preferred_element_type=F32
        ).astype(BF16)


def collect_kernel(m, tile_of, *refs):
    held, outs = refs[:4], refs[4:]
    p, c = position()
    for out, k in zip(outs, offsets(m)):
        tile = tile_of[2 * (p ^ k) + c]
        out[...] = pick(held, rank((tile // 2) ^ p, m), tile % 2 == c, slice(None))


def unpack_kernel(m, *refs):
    ga_ref, gb_ref = refs[m:]
    p, _ = position()
    r2, w = refs[0].shape
    for block, k in zip(refs, offsets(m)):
        cols = columns(p ^ k, w)
        ga_ref[0, :, cols] = block[0 : r2 // 2, :]
        gb_ref[0, :, cols] = block[r2 // 2 : r2, :]


def call(kernel, out_shape, in_specs, out_specs, params=PARAMS, **options):
    return pl.pallas_call(
        kernel,
        out_shape=out_shape,
        in_specs=in_specs,
        out_specs=out_specs,
        compiler_params=params,
        **options,
    )


def bf16(*shape):
    return jax.ShapeDtypeStruct(shape, BF16)


def shards(acts, cotangent, down, up, adapter_per_tile, adapter_storage_slot):
    groups, n = lax.axis_size("group"), lax.axis_size("fsdp")
    m, h = n // 2, n // 4
    _, r, d = down.shape

    def to_chip(k, block):
        pairs = [(2 * p + c, 2 * (p ^ k) + c) for p in range(m) for c in range(2)]
        return lax.ppermute(block, "fsdp", pairs)

    def to_device(x, k, block):
        pairs = [
            (g * n + 2 * p + c, (g ^ x) * n + 2 * (p ^ k) + c)
            for g in range(groups)
            for p in range(m)
            for c in range(2)
        ]
        return lax.ppermute(block, ("group", "fsdp"), pairs)

    def exchange(blocks):
        return [blocks[0]] + [to_chip(k, block) for block, k in zip(blocks[1:], offsets(m)[1:])]

    def with_other_core(*own):
        return [*own, *(lax.ppermute(half, "fsdp", [(f, f ^ 1) for f in range(n)]) for half in own)]

    def stack(blocks, *after):
        count = len(blocks) + len(after)
        return call(
            functools.partial(stack_kernel, h), bf16(h, *blocks[-1].shape), [VMEM] * count, VMEM
        )(*blocks, *after)

    ways = deliveries(groups, h)
    w = d // len(ways)
    flat = bf16(2 * r * w // LANES + ID_ROWS, LANES)
    first, *spread = call(
        functools.partial(pack_kernel, groups, h),
        [bf16(h // 2, *flat.shape)] + [flat] * h,
        [SMEM, SMEM, HBM, HBM],
        [HBM] * (h + 1),
        ALONE,
        scratch_shapes=[
            pltpu.VMEM((r, h * w), BF16),
            pltpu.VMEM((r, h * w), BF16),
            pltpu.VMEM((h, *flat.shape), BF16),
            pltpu.SemaphoreType.DMA((2, h)),
            pltpu.SemaphoreType.DMA((2, h)),
        ],
    )(adapter_per_tile, adapter_storage_slot, down, up)
    first = to_chip(h, first)
    near = [spread[0]] + [to_chip(k, spread[k]) for k in range(1, h)]
    handed = call(split_kernel, [flat] * (h // 2), [VMEM], [VMEM] * (h // 2))(first)
    far = [to_chip(h, near[0])] + [to_chip(k + 1, block) for k, block in enumerate(handed)]
    far += [to_chip(h, block) for block in near[h // 2 + 1 :]]
    near, marks = call(
        near_kernel, [bf16(h, *flat.shape), bf16(h, ID_ROWS, LANES)], [VMEM] * h, [VMEM] * 2
    )(*near)
    marks = [to_device(x, 0, marks) for x in range(1, groups)]
    held = with_other_core(near, stack(far, *marks))
    factors = call(
        functools.partial(deliver_kernel, groups),
        [bf16(2 * r, w)] * len(ways),
        [VMEM] * (groups + 3),
        [VMEM] * len(ways),
    )(*held, *marks)
    token = call(touch_kernel, jax.ShapeDtypeStruct((8, LANES), F32), [VMEM] * 2, VMEM)(
        factors[-1], cotangent
    )
    factors = [factors[0]] + [
        to_device(x, k, block) for (x, k), block in zip(ways[1:], factors[1:])
    ]
    tile_of = call(inverse_kernel, jax.ShapeDtypeStruct((n,), jnp.int32), [VMEM] * 4, SMEM)(*held)

    wide = bf16(2 * r, d // m)
    low, *parts = call(
        functools.partial(grads_kernel, m, groups),
        [bf16(r, acts.shape[0])] + [wide] * m,
        [VMEM] * (len(ways) + 3),
        [VMEM] * (m + 1),
    )(token, acts, cotangent, *factors)
    parts = exchange(parts)
    owned = call(functools.partial(collect_kernel, m), [wide] * m, [SMEM] + [VMEM] * 4, [VMEM] * m)(
        tile_of, *with_other_core(stack(parts[:h]), stack(parts[h:]))
    )
    grad_x = call(
        functools.partial(inputs_kernel, m, groups),
        bf16(*acts.shape),
        [VMEM] * (len(ways) + 2),
        VMEM,
        cost_estimate=pl.CostEstimate(
            flops=2 * r * acts.size, bytes_accessed=2 * acts.size, transcendentals=0
        ),
    )(owned[-1], low, *factors)
    grad_a, grad_b = call(
        functools.partial(unpack_kernel, m), [bf16(*down.shape)] * 2, [VMEM] * m, [VMEM] * 2
    )(*exchange(owned))
    return grad_x, grad_a, grad_b


def solution(mesh):
    placed = (
        P(("group", "fsdp"), None),
        P(("group", "fsdp"), None),
        P("fsdp", None, None),
        P("fsdp", None, None),
        P(("group", "fsdp")),
        P(),
    )
    return jax.shard_map(
        shards,
        mesh=mesh,
        in_specs=placed,
        out_specs=(
            P(("group", "fsdp"), None),
            P(("group", "fsdp"), None, None),
            P(("group", "fsdp"), None, None),
        ),
        check_vma=False,
    )
```

```python
import functools

import jax
import jax.numpy as jnp
from jax import lax
from jax.experimental import pallas as pl
from jax.experimental.pallas import tpu as pltpu
from jax.sharding import PartitionSpec as P

F32 = jnp.float32
BF16 = jnp.bfloat16
LANES = 128
ID_ROWS = 16
VMEM = pl.BlockSpec(memory_space=pltpu.VMEM)
HBM = pl.BlockSpec(memory_space=pltpu.HBM)
SMEM = pl.BlockSpec(memory_space=pltpu.SMEM)
PARAMS = pltpu.CompilerParams(vmem_limit_bytes=32 * 1024 * 1024)
ALONE = pltpu.CompilerParams(vmem_limit_bytes=60 * 1024 * 1024)


def position():
    me = lax.axis_index("fsdp")
    return me // 2, me % 2


def offsets(m):
    near, far = [*range(m // 2 - 1, 0, -1)], [*range(m - 1, m // 2 - 1, -1)]
    return [0, far[0], near[0], far[1], near[1], *far[2:], *near[2:]]


def rank(k, m):
    near = jnp.where(k > m // 2 - 3, m - 2 * k, m - k)
    near = jnp.where(k == 0, 0, near)
    far = jnp.where(k > m - 3, 2 * (m - 1 - k) + 1, m + 2 - k)
    return jnp.where(k < m // 2, near, far)


def deliveries(groups, h):
    pairs = [(x, k) for x in range(groups) for k in range(h)]
    far = sorted(pairs[1:], key=lambda pair: (-pair[0].bit_count() - pair[1].bit_count(), pair))
    return pairs[:1] + far


def share(groups, h, x, k):
    return (lax.axis_index("group") ^ x) * h + (lax.rem(position()[0], h) ^ k)


def columns(chunk, w):
    return pl.ds(pl.multiple_of(chunk * w, w), w)


def pack_kernel(groups, h, id_ref, storage_ref, down_hbm, up_hbm, *refs):
    outs, (down_ref, up_ref, out_ref, load_sems, store_sems) = refs[: h + 1], refs[h + 1 :]
    r, w = down_ref.shape[0], down_ref.shape[1] // h
    first = outs[0].shape[0]
    loads = []
    for k in range(h):
        cols = columns(share(groups, h, 0, k), w)
        loads.append(
            [
                pltpu.make_async_copy(src.at[0, :, cols], dst.at[:, k * w : (k + 1) * w], sem)
                for src, dst, sem in (
                    (down_hbm, down_ref, load_sems.at[0, k]),
                    (up_hbm, up_ref, load_sems.at[1, k]),
                )
            ]
        )
        for load in loads[-1]:
            load.start()
    mark = jnp.full((ID_ROWS, LANES), storage_ref[id_ref[0]].astype(F32), F32).astype(BF16)
    stores = []
    for k, pair in enumerate(loads):
        for load in pair:
            load.wait()
        for b in range(w // LANES):
            cols = slice(k * w + b * LANES, k * w + (b + 1) * LANES)
            out_ref[k, 2 * r * b : 2 * r * b + r, :] = down_ref[:, cols]
            out_ref[k, 2 * r * b + r : 2 * r * (b + 1), :] = up_ref[:, cols]
        out_ref[k, 2 * r * (w // LANES) :, :] = mark
        dsts = [outs[k + 1]] + ([outs[0].at[k - 1]] if 0 < k <= first else [])
        for i, dst in enumerate(dsts):
            stores.append(pltpu.make_async_copy(out_ref.at[k], dst, store_sems.at[i, k]))
            stores[-1].start()
    for store in stores:
        store.wait()


def stack_kernel(h, *refs):
    held_ref = refs[-1]
    for at, ref in enumerate(refs[:h]):
        held_ref[at] = ref[...]


def split_kernel(array_ref, *outs):
    for at, out in enumerate(outs):
        out[...] = array_ref[at]


def near_kernel(*refs):
    *blocks, held_ref, marks_ref = refs
    for at, ref in enumerate(blocks):
        block = ref[...]
        held_ref[at] = block
        marks_ref[at] = block[block.shape[0] - ID_ROWS :, :]


def pick(held, at, here, rows):
    own_a, own_b, other_a, other_b = held
    h = own_a.shape[0]
    in_a, at = at < h, lax.rem(at, h)
    own = jnp.where(in_a, own_a[at, rows, :], own_b[at, rows, :])
    other = jnp.where(in_a, other_a[at, rows, :], other_b[at, rows, :])
    return jnp.where(here, own, other)


def slots_of(held_ref):
    h, rows, _ = held_ref.shape
    return [
        held_ref[at, rows - ID_ROWS :, :].astype(F32)[0, 0].astype(jnp.int32) for at in range(h)
    ]


def deliver_kernel(groups, *refs):
    held, marks, outs = refs[:4], refs[4 : groups + 3], refs[groups + 3 :]
    p, c = position()
    h = held[0].shape[0]
    r2, w = outs[0].shape
    slots = [slots_of(held[0])] + [slots_of(mark) for mark in marks]
    for out, (x, k) in zip(outs, deliveries(groups, h)):
        slot = slots[x][k]
        for b in range(w // LANES):
            rows = slice(b * r2, (b + 1) * r2)
            out[:, b * LANES : (b + 1) * LANES] = pick(held, (slot // 2) ^ p, slot % 2 == c, rows)


def inverse_kernel(own_a, own_b, other_a, other_b, tile_of):
    p, c = position()
    for near, far, core in ((own_a, own_b, c), (other_a, other_b, 1 - c)):
        for k, slot in enumerate(slots_of(near) + slots_of(far)):
            tile_of[slot] = 2 * (p ^ k) + core


def touch_kernel(after, array, token_ref):
    token_ref[...] = jnp.zeros_like(token_ref)


def grads_kernel(m, groups, _, acts_ref, cot_ref, *refs):
    ways = deliveries(groups, m // 2)
    factors, low_ref, outs = refs[: len(ways)], refs[len(ways)], refs[len(ways) + 1 :]
    p, _ = position()
    r2, w = factors[0].shape
    r = r2 // 2
    rows = acts_ref.shape[0]
    dims_nt = (((1,), (1,)), ((), ()))
    low_u = jnp.zeros((rows, r), F32)
    low_h = jnp.zeros((rows, r), F32)
    for (x, k), factor in zip(ways, factors):
        cols = columns(share(groups, m // 2, x, k), w)
        low_u += lax.dot_general(acts_ref[:, cols], factor[0:r, :], dims_nt, preferred_element_type=F32)
        low_h += lax.dot_general(cot_ref[:, cols], factor[r:r2, :], dims_nt, preferred_element_type=F32)
    low_u = low_u.T.astype(BF16)
    low_h = low_h.T.astype(BF16)
    low_ref[...] = low_h
    for k, out in zip(offsets(m), outs):
        cols = columns(p ^ k, out.shape[1])
        out[0:r, :] = jnp.dot(low_h, acts_ref[:, cols], preferred_element_type=F32).astype(BF16)
        out[r:r2, :] = jnp.dot(low_u, cot_ref[:, cols], preferred_element_type=F32).astype(BF16)


def inputs_kernel(m, groups, _, low_ref, *refs):
    *factors, gx_ref = refs
    for (x, k), factor in zip(deliveries(groups, m // 2), factors):
        r2, w = factor.shape
        gx_ref[:, columns(share(groups, m // 2, x, k), w)] = lax.dot_general(
            low_ref[...], factor[0 : r2 // 2, :], (((0,), (0,)), ((), ())), preferred_element_type=F32
        ).astype(BF16)


def collect_kernel(m, tile_of, *refs):
    held, outs = refs[:4], refs[4:]
    p, c = position()
    for out, k in zip(outs, offsets(m)):
        tile = tile_of[2 * (p ^ k) + c]
        out[...] = pick(held, rank((tile // 2) ^ p, m), tile % 2 == c, slice(None))


def unpack_kernel(m, *refs):
    ga_ref, gb_ref = refs[m:]
    p, _ = position()
    r2, w = refs[0].shape
    for block, k in zip(refs, offsets(m)):
        cols = columns(p ^ k, w)
        ga_ref[0, :, cols] = block[0 : r2 // 2, :]
        gb_ref[0, :, cols] = block[r2 // 2 : r2, :]


def call(kernel, out_shape, in_specs, out_specs, params=PARAMS, **options):
    return pl.pallas_call(
        kernel,
        out_shape=out_shape,
        in_specs=in_specs,
        out_specs=out_specs,
        compiler_params=params,
        **options,
    )


def bf16(*shape):
    return jax.ShapeDtypeStruct(shape, BF16)


def shards(acts, cotangent, down, up, adapter_per_tile, adapter_storage_slot):
    groups, n = lax.axis_size("group"), lax.axis_size("fsdp")
    m, h = n // 2, n // 4
    _, r, d = down.shape

    def to_chip(k, block):
        pairs = [(2 * p + c, 2 * (p ^ k) + c) for p in range(m) for c in range(2)]
        return lax.ppermute(block, "fsdp", pairs)

    def to_device(x, k, block):
        pairs = [
            (g * n + 2 * p + c, (g ^ x) * n + 2 * (p ^ k) + c)
            for g in range(groups)
            for p in range(m)
            for c in range(2)
        ]
        return lax.ppermute(block, ("group", "fsdp"), pairs)

    def exchange(blocks):
        return [blocks[0]] + [to_chip(k, block) for block, k in zip(blocks[1:], offsets(m)[1:])]

    def with_other_core(*own):
        return [*own, *(lax.ppermute(half, "fsdp", [(f, f ^ 1) for f in range(n)]) for half in own)]

    def stack(blocks, *after):
        count = len(blocks) + len(after)
        return call(
            functools.partial(stack_kernel, h), bf16(h, *blocks[-1].shape), [VMEM] * count, VMEM
        )(*blocks, *after)

    ways = deliveries(groups, h)
    w = d // len(ways)
    flat = bf16(2 * r * w // LANES + ID_ROWS, LANES)
    first, *spread = call(
        functools.partial(pack_kernel, groups, h),
        [bf16(h // 2, *flat.shape)] + [flat] * h,
        [SMEM, SMEM, HBM, HBM],
        [HBM] * (h + 1),
        ALONE,
        scratch_shapes=[
            pltpu.VMEM((r, h * w), BF16),
            pltpu.VMEM((r, h * w), BF16),
            pltpu.VMEM((h, *flat.shape), BF16),
            pltpu.SemaphoreType.DMA((2, h)),
            pltpu.SemaphoreType.DMA((2, h)),
        ],
    )(adapter_per_tile, adapter_storage_slot, down, up)
    first = to_chip(h, first)
    near = [spread[0]] + [to_chip(k, spread[k]) for k in range(1, h)]
    handed = call(split_kernel, [flat] * (h // 2), [VMEM], [VMEM] * (h // 2))(first)
    far = [to_chip(h, near[0])] + [to_chip(k + 1, block) for k, block in enumerate(handed)]
    far += [to_chip(h, block) for block in near[h // 2 + 1 :]]
    near, marks = call(
        near_kernel, [bf16(h, *flat.shape), bf16(h, ID_ROWS, LANES)], [VMEM] * h, [VMEM] * 2
    )(*near)
    marks = [to_device(x, 0, marks) for x in range(1, groups)]
    held = with_other_core(near, stack(far, *marks))
    factors = call(
        functools.partial(deliver_kernel, groups),
        [bf16(2 * r, w)] * len(ways),
        [VMEM] * (groups + 3),
        [VMEM] * len(ways),
    )(*held, *marks)
    token = call(touch_kernel, jax.ShapeDtypeStruct((8, LANES), F32), [VMEM] * 2, VMEM)(
        factors[-1], cotangent
    )
    factors = [factors[0]] + [
        to_device(x, k, block) for (x, k), block in zip(ways[1:], factors[1:])
    ]
    tile_of = call(inverse_kernel, jax.ShapeDtypeStruct((n,), jnp.int32), [VMEM] * 4, SMEM)(*held)

    wide = bf16(2 * r, d // m)
    low, *parts = call(
        functools.partial(grads_kernel, m, groups),
        [bf16(r, acts.shape[0])] + [wide] * m,
        [VMEM] * (len(ways) + 3),
        [VMEM] * (m + 1),
    )(token, acts, cotangent, *factors)
    parts = exchange(parts)
    owned = call(functools.partial(collect_kernel, m), [wide] * m, [SMEM] + [VMEM] * 4, [VMEM] * m)(
        tile_of, *with_other_core(stack(parts[:h]), stack(parts[h:]))
    )
    grad_x = call(
        functools.partial(inputs_kernel, m, groups),
        bf16(*acts.shape),
        [VMEM] * (len(ways) + 2),
        VMEM,
        cost_estimate=pl.CostEstimate(
            flops=2 * r * acts.size, bytes_accessed=2 * acts.size, transcendentals=0
        ),
    )(owned[-1], low, *factors)
    grad_a, grad_b = call(
        functools.partial(unpack_kernel, m), [bf16(*down.shape)] * 2, [VMEM] * m, [VMEM] * 2
    )(*exchange(owned))
    return grad_x, grad_a, grad_b


def solution(mesh):
    placed = (
        P(("group", "fsdp"), None),
        P(("group", "fsdp"), None),
        P("fsdp", None, None),
        P("fsdp", None, None),
        P(("group", "fsdp")),
        P(),
    )
    return jax.shard_map(
        shards,
        mesh=mesh,
        in_specs=placed,
        out_specs=(
            P(("group", "fsdp"), None),
            P(("group", "fsdp"), None, None),
            P(("group", "fsdp"), None, None),
        ),
        check_vma=False,
    )
```

```python
import functools

import jax
import jax.numpy as jnp
from jax import lax
from jax.experimental import pallas as pl
from jax.experimental.pallas import tpu as pltpu
from jax.sharding import PartitionSpec as P

F32 = jnp.float32
BF16 = jnp.bfloat16
LANES = 128
ID_ROWS = 16
VMEM = pl.BlockSpec(memory_space=pltpu.VMEM)
HBM = pl.BlockSpec(memory_space=pltpu.HBM)
SMEM = pl.BlockSpec(memory_space=pltpu.SMEM)
PARAMS = pltpu.CompilerParams(vmem_limit_bytes=32 * 1024 * 1024)
ALONE = pltpu.CompilerParams(vmem_limit_bytes=60 * 1024 * 1024)


def position():
    me = lax.axis_index("fsdp")
    return me // 2, me % 2


def offsets(m):
    near, far = [*range(m // 2 - 1, 0, -1)], [*range(m - 1, m // 2 - 1, -1)]
    return [0, far[0], near[0], far[1], near[1], *far[2:], *near[2:]]


def rank(k, m):
    near = jnp.where(k > m // 2 - 3, m - 2 * k, m - k)
    near = jnp.where(k == 0, 0, near)
    far = jnp.where(k > m - 3, 2 * (m - 1 - k) + 1, m + 2 - k)
    return jnp.where(k < m // 2, near, far)


def deliveries(groups, h):
    pairs = [(x, k) for x in range(groups) for k in range(h)]
    far = sorted(pairs[1:], key=lambda pair: (-pair[0].bit_count() - pair[1].bit_count(), pair))
    return pairs[:1] + far


def share(groups, h, x, k):
    return (lax.axis_index("group") ^ x) * h + (lax.rem(position()[0], h) ^ k)


def columns(chunk, w):
    return pl.ds(pl.multiple_of(chunk * w, w), w)


def pack_kernel(groups, h, id_ref, storage_ref, down_hbm, up_hbm, *refs):
    outs, (down_ref, up_ref, out_ref, load_sems, store_sems) = refs[: h + 1], refs[h + 1 :]
    r, w = down_ref.shape[0], down_ref.shape[1] // h
    first = outs[0].shape[0]
    loads = []
    for k in range(h):
        cols = columns(share(groups, h, 0, k), w)
        loads.append(
            [
                pltpu.make_async_copy(src.at[0, :, cols], dst.at[:, k * w : (k + 1) * w], sem)
                for src, dst, sem in (
                    (down_hbm, down_ref, load_sems.at[0, k]),
                    (up_hbm, up_ref, load_sems.at[1, k]),
                )
            ]
        )
        for load in loads[-1]:
            load.start()
    mark = jnp.full((ID_ROWS, LANES), storage_ref[id_ref[0]].astype(F32), F32).astype(BF16)
    stores = []
    for k, pair in enumerate(loads):
        for load in pair:
            load.wait()
        for b in range(w // LANES):
            cols = slice(k * w + b * LANES, k * w + (b + 1) * LANES)
            out_ref[k, 2 * r * b : 2 * r * b + r, :] = down_ref[:, cols]
            out_ref[k, 2 * r * b + r : 2 * r * (b + 1), :] = up_ref[:, cols]
        out_ref[k, 2 * r * (w // LANES) :, :] = mark
        dsts = [outs[k + 1]] + ([outs[0].at[k - 1]] if 0 < k <= first else [])
        for i, dst in enumerate(dsts):
            stores.append(pltpu.make_async_copy(out_ref.at[k], dst, store_sems.at[i, k]))
            stores[-1].start()
    for store in stores:
        store.wait()


def stack_kernel(h, *refs):
    held_ref = refs[-1]
    for at, ref in enumerate(refs[:h]):
        held_ref[at] = ref[...]


def split_kernel(array_ref, *outs):
    for at, out in enumerate(outs):
        out[...] = array_ref[at]


def marks_kernel(id_ref, storage_ref, *refs):
    *blocks, marks_ref = refs
    mark = jnp.full((ID_ROWS, LANES), storage_ref[id_ref[0]].astype(F32), F32).astype(BF16)
    marks_ref[0] = mark
    for at, block in enumerate(blocks):
        marks_ref[at + 1] = block[block.shape[0] - ID_ROWS :, :]


def pick(held, at, here, rows):
    own_a, own_b, other_a, other_b = held
    h = own_a.shape[0]
    in_a, at = at < h, lax.rem(at, h)
    own = jnp.where(in_a, own_a[at, rows, :], own_b[at, rows, :])
    other = jnp.where(in_a, other_a[at, rows, :], other_b[at, rows, :])
    return jnp.where(here, own, other)


def slots_of(held_ref):
    h, rows, _ = held_ref.shape
    return [
        held_ref[at, rows - ID_ROWS :, :].astype(F32)[0, 0].astype(jnp.int32) for at in range(h)
    ]


def deliver_kernel(groups, *refs):
    held, marks, outs = refs[:4], refs[4 : groups + 3], refs[groups + 3 :]
    p, c = position()
    h = held[0].shape[0]
    r2, w = outs[0].shape
    slots = [slots_of(held[0])] + [slots_of(mark) for mark in marks]
    for out, (x, k) in zip(outs, deliveries(groups, h)):
        slot = slots[x][k]
        for b in range(w // LANES):
            rows = slice(b * r2, (b + 1) * r2)
            out[:, b * LANES : (b + 1) * LANES] = pick(held, (slot // 2) ^ p, slot % 2 == c, rows)


def inverse_kernel(m, own_a, own_b, other_a, other_b, plan_ref, tile_of):
    p, c = position()
    for near, far, core in ((own_a, own_b, c), (other_a, other_b, 1 - c)):
        for k, slot in enumerate(slots_of(near) + slots_of(far)):
            tile_of[slot] = 2 * (p ^ k) + core
    for i, k in enumerate(offsets(m)):
        plan_ref[i] = jnp.full(plan_ref.shape[1:], tile_of[2 * (p ^ k) + c], jnp.int32)


def touch_kernel(after, array, token_ref):
    token_ref[...] = jnp.zeros_like(token_ref)


def grads_kernel(m, groups, _, acts_ref, cot_ref, *refs):
    ways = deliveries(groups, m // 2)
    factors, low_ref, outs = refs[: len(ways)], refs[len(ways)], refs[len(ways) + 1 :]
    p, _ = position()
    r2, w = factors[0].shape
    r = r2 // 2
    rows = acts_ref.shape[0]
    dims_nt = (((1,), (1,)), ((), ()))
    low_u = jnp.zeros((rows, r), F32)
    low_h = jnp.zeros((rows, r), F32)
    for (x, k), factor in zip(ways, factors):
        cols = columns(share(groups, m // 2, x, k), w)
        low_u += lax.dot_general(acts_ref[:, cols], factor[0:r, :], dims_nt, preferred_element_type=F32)
        low_h += lax.dot_general(cot_ref[:, cols], factor[r:r2, :], dims_nt, preferred_element_type=F32)
    low_u = low_u.T.astype(BF16)
    low_h = low_h.T.astype(BF16)
    low_ref[...] = low_h
    for k, out in zip(offsets(m), outs):
        cols = columns(p ^ k, out.shape[1])
        out[0:r, :] = jnp.dot(low_h, acts_ref[:, cols], preferred_element_type=F32).astype(BF16)
        out[r:r2, :] = jnp.dot(low_u, cot_ref[:, cols], preferred_element_type=F32).astype(BF16)


def inputs_kernel(m, groups, _, low_ref, *refs):
    *factors, gx_ref = refs
    for (x, k), factor in zip(deliveries(groups, m // 2), factors):
        r2, w = factor.shape
        gx_ref[:, columns(share(groups, m // 2, x, k), w)] = lax.dot_general(
            low_ref[...], factor[0 : r2 // 2, :], (((0,), (0,)), ((), ())), preferred_element_type=F32
        ).astype(BF16)


def collect_kernel(m, plan_ref, *refs):
    held, outs = refs[:4], refs[4:]
    p, c = position()
    tiles = [plan_ref[i][0, 0] for i in range(m)]
    for out, tile in zip(outs, tiles):
        out[...] = pick(held, rank((tile // 2) ^ p, m), tile % 2 == c, slice(None))


def unpack_kernel(m, *refs):
    ga_ref, gb_ref = refs[m:]
    p, _ = position()
    r2, w = refs[0].shape
    for block, k in zip(refs, offsets(m)):
        cols = columns(p ^ k, w)
        ga_ref[0, :, cols] = block[0 : r2 // 2, :]
        gb_ref[0, :, cols] = block[r2 // 2 : r2, :]


def call(kernel, out_shape, in_specs, out_specs, params=PARAMS, **options):
    return pl.pallas_call(
        kernel,
        out_shape=out_shape,
        in_specs=in_specs,
        out_specs=out_specs,
        compiler_params=params,
        **options,
    )


def bf16(*shape):
    return jax.ShapeDtypeStruct(shape, BF16)


def shards(acts, cotangent, down, up, adapter_per_tile, adapter_storage_slot):
    groups, n = lax.axis_size("group"), lax.axis_size("fsdp")
    m, h = n // 2, n // 4
    _, r, d = down.shape

    def to_chip(k, block):
        pairs = [(2 * p + c, 2 * (p ^ k) + c) for p in range(m) for c in range(2)]
        return lax.ppermute(block, "fsdp", pairs)

    def to_device(x, k, block):
        pairs = [
            (g * n + 2 * p + c, (g ^ x) * n + 2 * (p ^ k) + c)
            for g in range(groups)
            for p in range(m)
            for c in range(2)
        ]
        return lax.ppermute(block, ("group", "fsdp"), pairs)

    def exchange(blocks):
        return [blocks[0]] + [to_chip(k, block) for block, k in zip(blocks[1:], offsets(m)[1:])]

    def with_other_core(*own):
        return [*own, *(lax.ppermute(half, "fsdp", [(f, f ^ 1) for f in range(n)]) for half in own)]

    def stack(blocks, *after):
        count = len(blocks) + len(after)
        return call(
            functools.partial(stack_kernel, h), bf16(h, *blocks[-1].shape), [VMEM] * count, VMEM
        )(*blocks, *after)

    ways = deliveries(groups, h)
    w = d // len(ways)
    flat = bf16(2 * r * w // LANES + ID_ROWS, LANES)
    first, *spread = call(
        functools.partial(pack_kernel, groups, h),
        [bf16(h // 2, *flat.shape)] + [flat] * h,
        [SMEM, SMEM, HBM, HBM],
        [HBM] * (h + 1),
        ALONE,
        scratch_shapes=[
            pltpu.VMEM((r, h * w), BF16),
            pltpu.VMEM((r, h * w), BF16),
            pltpu.VMEM((h, *flat.shape), BF16),
            pltpu.SemaphoreType.DMA((2, h)),
            pltpu.SemaphoreType.DMA((2, h)),
        ],
    )(adapter_per_tile, adapter_storage_slot, down, up)
    first = to_chip(h, first)
    near = [spread[0]] + [to_chip(k, spread[k]) for k in range(1, h)]
    handed = call(split_kernel, [flat] * (h // 2), [VMEM], [VMEM] * (h // 2))(first)
    far = [to_chip(h, near[0])] + [to_chip(k + 1, block) for k, block in enumerate(handed)]
    far += [to_chip(h, block) for block in near[h // 2 + 1 :]]
    marks = call(
        marks_kernel, bf16(h, ID_ROWS, LANES), [SMEM] * 2 + [VMEM] * (h - 1), VMEM
    )(adapter_per_tile, adapter_storage_slot, *near[1:])
    marks = [to_device(x, 0, marks) for x in range(1, groups)]
    held = with_other_core(stack(near), stack(far, *marks))
    factors = call(
        functools.partial(deliver_kernel, groups),
        [bf16(2 * r, w)] * len(ways),
        [VMEM] * (groups + 3),
        [VMEM] * len(ways),
    )(*held, *marks)
    token = call(touch_kernel, jax.ShapeDtypeStruct((8, LANES), F32), [VMEM] * 2, VMEM)(
        factors[-1], cotangent
    )
    factors = [factors[0]] + [
        to_device(x, k, block) for (x, k), block in zip(ways[1:], factors[1:])
    ]
    plan = call(
        functools.partial(inverse_kernel, m),
        jax.ShapeDtypeStruct((m, 8, LANES), jnp.int32),
        [VMEM] * 4,
        VMEM,
        scratch_shapes=[pltpu.SMEM((n,), jnp.int32)],
    )(*held)

    wide = bf16(2 * r, d // m)
    low, *parts = call(
        functools.partial(grads_kernel, m, groups),
        [bf16(r, acts.shape[0])] + [wide] * m,
        [VMEM] * (len(ways) + 3),
        [VMEM] * (m + 1),
    )(token, acts, cotangent, *factors)
    parts = exchange(parts)
    owned = call(functools.partial(collect_kernel, m), [wide] * m, [VMEM] * 5, [VMEM] * m)(
        plan, *with_other_core(stack(parts[:h]), stack(parts[h:]))
    )
    grad_x = call(
        functools.partial(inputs_kernel, m, groups),
        bf16(*acts.shape),
        [VMEM] * (len(ways) + 2),
        VMEM,
        cost_estimate=pl.CostEstimate(
            flops=2 * r * acts.size, bytes_accessed=2 * acts.size, transcendentals=0
        ),
    )(owned[-1], low, *factors)
    grad_a, grad_b = call(
        functools.partial(unpack_kernel, m), [bf16(*down.shape)] * 2, [VMEM] * m, [VMEM] * 2
    )(*exchange(owned))
    return grad_x, grad_a, grad_b


def solution(mesh):
    placed = (
        P(("group", "fsdp"), None),
        P(("group", "fsdp"), None),
        P("fsdp", None, None),
        P("fsdp", None, None),
        P(("group", "fsdp")),
        P(),
    )
    return jax.shard_map(
        shards,
        mesh=mesh,
        in_specs=placed,
        out_specs=(
            P(("group", "fsdp"), None),
            P(("group", "fsdp"), None, None),
            P(("group", "fsdp"), None, None),
        ),
        check_vma=False,
    )
```

```python
import functools

import jax
import jax.numpy as jnp
from jax import lax
from jax.experimental import pallas as pl
from jax.experimental.pallas import tpu as pltpu
from jax.sharding import PartitionSpec as P

F32 = jnp.float32
BF16 = jnp.bfloat16
LANES = 128
ID_ROWS = 16
VMEM = pl.BlockSpec(memory_space=pltpu.VMEM)
HBM = pl.BlockSpec(memory_space=pltpu.HBM)
SMEM = pl.BlockSpec(memory_space=pltpu.SMEM)
PARAMS = pltpu.CompilerParams(vmem_limit_bytes=32 * 1024 * 1024)
ALONE = pltpu.CompilerParams(vmem_limit_bytes=60 * 1024 * 1024)


def position():
    me = lax.axis_index("fsdp")
    return me // 2, me % 2


def offsets(m):
    near, far = [*range(m // 2 - 1, 0, -1)], [*range(m - 1, m // 2 - 1, -1)]
    return [0, far[0], near[0], far[1], near[1], *far[2:], *near[2:]]


def rank(k, m):
    near = jnp.where(k > m // 2 - 3, m - 2 * k, m - k)
    near = jnp.where(k == 0, 0, near)
    far = jnp.where(k > m - 3, 2 * (m - 1 - k) + 1, m + 2 - k)
    return jnp.where(k < m // 2, near, far)


def deliveries(groups, h):
    pairs = [(x, k) for x in range(groups) for k in range(h)]
    far = sorted(pairs[1:], key=lambda pair: (-pair[0].bit_count() - pair[1].bit_count(), pair))
    return pairs[:1] + far


def share(groups, h, x, k):
    return (lax.axis_index("group") ^ x) * h + (lax.rem(position()[0], h) ^ k)


def columns(chunk, w):
    return pl.ds(pl.multiple_of(chunk * w, w), w)


def pack_kernel(groups, h, id_ref, storage_ref, down_hbm, up_hbm, *refs):
    outs, (down_ref, up_ref, out_ref, load_sems, store_sems) = refs[: h + 1], refs[h + 1 :]
    r, w = down_ref.shape[0], down_ref.shape[1] // h
    first = outs[0].shape[0]
    loads = []
    for k in range(h):
        cols = columns(share(groups, h, 0, k), w)
        loads.append(
            [
                pltpu.make_async_copy(src.at[0, :, cols], dst.at[:, k * w : (k + 1) * w], sem)
                for src, dst, sem in (
                    (down_hbm, down_ref, load_sems.at[0, k]),
                    (up_hbm, up_ref, load_sems.at[1, k]),
                )
            ]
        )
        for load in loads[-1]:
            load.start()
    mark = jnp.full((ID_ROWS, LANES), storage_ref[id_ref[0]].astype(F32), F32).astype(BF16)
    stores = []
    for k, pair in enumerate(loads):
        for load in pair:
            load.wait()
        for b in range(w // LANES):
            cols = slice(k * w + b * LANES, k * w + (b + 1) * LANES)
            out_ref[k, 2 * r * b : 2 * r * b + r, :] = down_ref[:, cols]
            out_ref[k, 2 * r * b + r : 2 * r * (b + 1), :] = up_ref[:, cols]
        out_ref[k, 2 * r * (w // LANES) :, :] = mark
        dsts = [outs[k + 1]] + ([outs[0].at[k - 1]] if 0 < k <= first else [])
        for i, dst in enumerate(dsts):
            stores.append(pltpu.make_async_copy(out_ref.at[k], dst, store_sems.at[i, k]))
            stores[-1].start()
    for store in stores:
        store.wait()


def stack_kernel(h, *refs):
    held_ref = refs[-1]
    for at, ref in enumerate(refs[:h]):
        held_ref[at] = ref[...]


def split_kernel(_, array_ref, *outs):
    for at, out in enumerate(outs):
        out[...] = array_ref[at]


def marks_kernel(*refs):
    *blocks, marks_ref = refs
    for at, block in enumerate(blocks):
        marks_ref[at] = block[block.shape[0] - ID_ROWS :, :]


def copy_kernel(in_ref, out_ref):
    out_ref[...] = in_ref[...]


def pick(held, at, here, rows):
    own_a, own_b, other_a, other_b = held
    h = own_a.shape[0]
    in_a, at = at < h, lax.rem(at, h)
    own = jnp.where(in_a, own_a[at, rows, :], own_b[at, rows, :])
    other = jnp.where(in_a, other_a[at, rows, :], other_b[at, rows, :])
    return jnp.where(here, own, other)


def slots_of(held_ref):
    h, rows, _ = held_ref.shape
    return [
        held_ref[at, rows - ID_ROWS :, :].astype(F32)[0, 0].astype(jnp.int32) for at in range(h)
    ]


def deliver_kernel(groups, *refs):
    held, marks, outs = refs[:4], refs[4 : groups + 3], refs[groups + 3 :]
    p, c = position()
    h = held[0].shape[0]
    r2, w = outs[0].shape
    slots = [slots_of(held[0])] + [slots_of(mark) for mark in marks]
    for out, (x, k) in zip(outs, deliveries(groups, h)):
        slot = slots[x][k]
        for b in range(w // LANES):
            rows = slice(b * r2, (b + 1) * r2)
            out[:, b * LANES : (b + 1) * LANES] = pick(held, (slot // 2) ^ p, slot % 2 == c, rows)


def inverse_kernel(m, own_a, own_b, other_a, other_b, plan_ref, tile_of):
    p, c = position()
    for near, far, core in ((own_a, own_b, c), (other_a, other_b, 1 - c)):
        for k, slot in enumerate(slots_of(near) + slots_of(far)):
            tile_of[slot] = 2 * (p ^ k) + core
    for i, k in enumerate(offsets(m)):
        plan_ref[i] = jnp.full(plan_ref.shape[1:], tile_of[2 * (p ^ k) + c], jnp.int32)


def touch_kernel(after, array, token_ref):
    token_ref[...] = jnp.zeros_like(token_ref)


def grads_kernel(m, groups, _, acts_ref, cot_ref, *refs):
    ways = deliveries(groups, m // 2)
    factors, low_ref, outs = refs[: len(ways)], refs[len(ways)], refs[len(ways) + 1 :]
    p, _ = position()
    r2, w = factors[0].shape
    r = r2 // 2
    rows = acts_ref.shape[0]
    dims_nt = (((1,), (1,)), ((), ()))
    low_u = jnp.zeros((rows, r), F32)
    low_h = jnp.zeros((rows, r), F32)
    for (x, k), factor in zip(ways, factors):
        cols = columns(share(groups, m // 2, x, k), w)
        low_u += lax.dot_general(acts_ref[:, cols], factor[0:r, :], dims_nt, preferred_element_type=F32)
        low_h += lax.dot_general(cot_ref[:, cols], factor[r:r2, :], dims_nt, preferred_element_type=F32)
    low_u = low_u.T.astype(BF16)
    low_h = low_h.T.astype(BF16)
    low_ref[...] = low_h
    for k, out in zip(offsets(m), outs):
        cols = columns(p ^ k, out.shape[1])
        out[0:r, :] = jnp.dot(low_h, acts_ref[:, cols], preferred_element_type=F32).astype(BF16)
        out[r:r2, :] = jnp.dot(low_u, cot_ref[:, cols], preferred_element_type=F32).astype(BF16)


def inputs_kernel(m, groups, _, low_ref, *refs):
    *factors, gx_ref = refs
    for (x, k), factor in zip(deliveries(groups, m // 2), factors):
        r2, w = factor.shape
        gx_ref[:, columns(share(groups, m // 2, x, k), w)] = lax.dot_general(
            low_ref[...], factor[0 : r2 // 2, :], (((0,), (0,)), ((), ())), preferred_element_type=F32
        ).astype(BF16)


def collect_kernel(m, plan_ref, *refs):
    held, outs = refs[:4], refs[4:]
    p, c = position()
    tiles = [plan_ref[i][0, 0] for i in range(m)]
    for out, tile in zip(outs, tiles):
        out[...] = pick(held, rank((tile // 2) ^ p, m), tile % 2 == c, slice(None))


def unpack_kernel(m, *refs):
    ga_ref, gb_ref = refs[m:]
    p, _ = position()
    r2, w = refs[0].shape
    for block, k in zip(refs, offsets(m)):
        cols = columns(p ^ k, w)
        ga_ref[0, :, cols] = block[0 : r2 // 2, :]
        gb_ref[0, :, cols] = block[r2 // 2 : r2, :]


def call(kernel, out_shape, in_specs, out_specs, params=PARAMS, **options):
    return pl.pallas_call(
        kernel,
        out_shape=out_shape,
        in_specs=in_specs,
        out_specs=out_specs,
        compiler_params=params,
        **options,
    )


def bf16(*shape):
    return jax.ShapeDtypeStruct(shape, BF16)


def shards(acts, cotangent, down, up, adapter_per_tile, adapter_storage_slot):
    groups, n = lax.axis_size("group"), lax.axis_size("fsdp")
    m, h = n // 2, n // 4
    _, r, d = down.shape

    def to_chip(k, block):
        pairs = [(2 * p + c, 2 * (p ^ k) + c) for p in range(m) for c in range(2)]
        return lax.ppermute(block, "fsdp", pairs)

    def to_device(x, k, block):
        pairs = [
            (g * n + 2 * p + c, (g ^ x) * n + 2 * (p ^ k) + c)
            for g in range(groups)
            for p in range(m)
            for c in range(2)
        ]
        return lax.ppermute(block, ("group", "fsdp"), pairs)

    def exchange(blocks):
        return [blocks[0]] + [to_chip(k, block) for block, k in zip(blocks[1:], offsets(m)[1:])]

    def with_other_core(*own):
        return [*own, *(lax.ppermute(half, "fsdp", [(f, f ^ 1) for f in range(n)]) for half in own)]

    def stack(blocks, *after):
        count = len(blocks) + len(after)
        return call(
            functools.partial(stack_kernel, h), bf16(h, *blocks[-1].shape), [VMEM] * count, VMEM
        )(*blocks, *after)

    ways = deliveries(groups, h)
    w = d // len(ways)
    flat = bf16(2 * r * w // LANES + ID_ROWS, LANES)
    first, *spread = call(
        functools.partial(pack_kernel, groups, h),
        [bf16(h // 2, *flat.shape)] + [flat] * h,
        [SMEM, SMEM, HBM, HBM],
        [HBM] * (h + 1),
        ALONE,
        scratch_shapes=[
            pltpu.VMEM((r, h * w), BF16),
            pltpu.VMEM((r, h * w), BF16),
            pltpu.VMEM((h, *flat.shape), BF16),
            pltpu.SemaphoreType.DMA((2, h)),
            pltpu.SemaphoreType.DMA((2, h)),
        ],
    )(adapter_per_tile, adapter_storage_slot, down, up)
    first = to_chip(h, first)
    near = [spread[0]] + [to_chip(k, spread[k]) for k in range(1, h)]
    own = call(copy_kernel, flat, [VMEM], VMEM)(near[0])
    handed = call(split_kernel, [flat] * (h // 2), [VMEM] * 2, [VMEM] * (h // 2))(own, first)
    far = [to_chip(h, near[0])] + [to_chip(k + 1, block) for k, block in enumerate(handed)]
    far += [to_chip(h, block) for block in near[h // 2 + 1 :]]
    near[0] = own
    marks = call(marks_kernel, bf16(h, ID_ROWS, LANES), [VMEM] * h, VMEM)(*near)
    marks = [to_device(x, 0, marks) for x in range(1, groups)]
    held = with_other_core(stack(near), stack(far, *marks))
    factors = call(
        functools.partial(deliver_kernel, groups),
        [bf16(2 * r, w)] * len(ways),
        [VMEM] * (groups + 3),
        [VMEM] * len(ways),
    )(*held, *marks)
    token = call(touch_kernel, jax.ShapeDtypeStruct((8, LANES), F32), [VMEM] * 2, VMEM)(
        factors[-1], cotangent
    )
    factors = [factors[0]] + [
        to_device(x, k, block) for (x, k), block in zip(ways[1:], factors[1:])
    ]
    plan = call(
        functools.partial(inverse_kernel, m),
        jax.ShapeDtypeStruct((m, 8, LANES), jnp.int32),
        [VMEM] * 4,
        VMEM,
        scratch_shapes=[pltpu.SMEM((n,), jnp.int32)],
    )(*held)

    wide = bf16(2 * r, d // m)
    low, *parts = call(
        functools.partial(grads_kernel, m, groups),
        [bf16(r, acts.shape[0])] + [wide] * m,
        [VMEM] * (len(ways) + 3),
        [VMEM] * (m + 1),
    )(token, acts, cotangent, *factors)
    parts = exchange(parts)
    owned = call(functools.partial(collect_kernel, m), [wide] * m, [VMEM] * 5, [VMEM] * m)(
        plan, *with_other_core(stack(parts[:h]), stack(parts[h:]))
    )
    grad_x = call(
        functools.partial(inputs_kernel, m, groups),
        bf16(*acts.shape),
        [VMEM] * (len(ways) + 2),
        VMEM,
        cost_estimate=pl.CostEstimate(
            flops=2 * r * acts.size, bytes_accessed=2 * acts.size, transcendentals=0
        ),
    )(owned[-1], low, *factors)
    grad_a, grad_b = call(
        functools.partial(unpack_kernel, m), [bf16(*down.shape)] * 2, [VMEM] * m, [VMEM] * 2
    )(*exchange(owned))
    return grad_x, grad_a, grad_b


def solution(mesh):
    placed = (
        P(("group", "fsdp"), None),
        P(("group", "fsdp"), None),
        P("fsdp", None, None),
        P("fsdp", None, None),
        P(("group", "fsdp")),
        P(),
    )
    return jax.shard_map(
        shards,
        mesh=mesh,
        in_specs=placed,
        out_specs=(
            P(("group", "fsdp"), None),
            P(("group", "fsdp"), None, None),
            P(("group", "fsdp"), None, None),
        ),
        check_vma=False,
    )
```
